128 devices in a mesh: pipe: 2 (over core), ctx: 8 (over x, z_lo), tp: 8 (over y, z_hi).
Axes of the slice: x: 4, y: 4, z: 4 (z_hi: 2, z_lo: 2; z = z_hi * 2 + z_lo), core: 2. Of those that a mesh axis runs over, the one named last changes fastest.
Arguments:
- latents: float32 [3, 1024, 1024], P(None, 'ctx'), may hold values from -6 to 6
- cotangent: float32 [3, 1024, 1024], P(None, 'ctx'), may hold values from -6 to 6
- labels: int32 [3], replicated, may hold values from 0 to 999
- steps: int32 [3], replicated, may hold values from 0 to 999
- label_table: bfloat16 [1000, 1024], replicated, may hold values from -5 to 5
- w_ada: bfloat16 [2, 1024, 6, 1024], P('pipe', None, None, ('ctx', 'tp')), may hold values from -0.1875 to 0.1875
- w_qkv: bfloat16 [2, 1024, 3, 1024], P('pipe', 'ctx', None, 'tp'), may hold values from -0.1875 to 0.1875
- w_out: bfloat16 [2, 1024, 1024], P('pipe', 'tp', 'ctx'), may hold values from -0.75 to 0.75
- w_up: bfloat16 [2, 1024, 4096], P('pipe', 'ctx', 'tp'), may hold values from -0.1875 to 0.1875
- w_down: bfloat16 [2, 4096, 1024], P('pipe', 'tp', 'ctx'), may hold values from -0.09375 to 0.09375
Outputs:
- ends: float32 [2, 3, 1024, 1024], P('pipe', None, 'ctx')
- grad_table: float32 [1000, 1024], replicated
- grad_ada: float32 [2, 1024, 6, 1024], P('pipe', None, None, ('ctx', 'tp'))
- grad_qkv: float32 [2, 1024, 3, 1024], P('pipe', 'ctx', None, 'tp')
- grad_out: float32 [2, 1024, 1024], P('pipe', 'tp', 'ctx')
- grad_up: float32 [2, 1024, 4096], P('pipe', 'ctx', 'tp')
- grad_down: float32 [2, 4096, 1024], P('pipe', 'tp', 'ctx')
The draws below stay inside these ranges and needn't reach their ends.
All inputs are finite; a program needn't handle non-finite values.
Results may differ from the reference program's by a relative error of at most 0.025.
Values may be sent and summed in bfloat16 or wider, within the bound.
No kernel may reach another device: no remote copies, remote signals or barrier semaphores. Data moves between devices by JAX's collectives and lax.ppermute only.
A program may use at most 128 MiB of HBM per device.

```python
import math
import jax
import jax.numpy as jnp
from jax import lax

D = 1024
HEADS = 16
HEAD_DIM = 64
FF = 4096
CLASSES = 1000
TIMESTEPS = 1000
LAYERS = 2
SEQ = 1024
LATENTS = 3


def draw_cotangent(key, part):
    key = jax.random.fold_in(key, 11)
    common_key = jax.random.fold_in(key, 1)
    noise_key = jax.random.fold_in(key, 2)
    common = jax.random.normal(common_key, (LATENTS, 1, D), jnp.float32)
    noise = jax.random.normal(noise_key, (LATENTS, SEQ, D), jnp.float32)
    values = 0.9 * common + 0.45 * noise
    return jnp.clip(values, -6.0, 6.0).astype(jnp.float32)


def steps_of(own_key, shape, pieces, least, high):
    factor_of, own = 1.0, jax.random.fold_in(own_key, 6)
    for axis_at, parts in pieces:
        heights = jnp.exp(jax.random.uniform(jax.random.fold_in(own, axis_at), (parts,), jnp.float32, least / len(pieces), high / len(pieces)))
        factor_of = factor_of * jnp.repeat(heights, shape[axis_at] // parts).reshape([-1 if axis == axis_at else 1 for axis in range(len(shape))])
    return factor_of


def bell_draw(stream_key, extent, scale, limit, split=(), kind=jnp.bfloat16):
    drawn = jax.random.normal(stream_key, extent, jnp.float32) * scale
    if len(split) > 0:
        drawn = steps_of(stream_key, extent, split, -0.22, 0.18) * drawn
    return jnp.clip(drawn, min=-limit, max=limit).astype(kind)


def setup_inputs(seed: int = 0) -> dict:
    arg_keys = jax.random.split(jax.random.key(seed), 11)
    return {
        "latents": bell_draw(arg_keys[0], (LATENTS, SEQ, D), 1.0, 6.0, ((1, 8),), jnp.float32),
        "cotangent": draw_cotangent(jax.random.fold_in(arg_keys[10], 71), 0),
        "labels": jax.random.randint(arg_keys[2], (LATENTS,), 0, CLASSES).astype(jnp.int32),
        "steps": jax.random.randint(arg_keys[3], (LATENTS,), 0, TIMESTEPS).astype(jnp.int32),
        "label_table": bell_draw(arg_keys[4], (CLASSES, D), 0.8, 5.0),
        "w_ada": bell_draw(arg_keys[5], (LAYERS, D, 6, D), D ** -0.5, 0.1875, ((0, 2), (3, 64))),
        "w_qkv": bell_draw(arg_keys[6], (LAYERS, D, 3, D), D ** -0.5, 0.1875, ((0, 2), (1, 8), (3, 8))),
        "w_out": bell_draw(arg_keys[7], (LAYERS, D, D), (D // 16) ** -0.5, 0.75, ((0, 2), (1, 8), (2, 8))),
        "w_up": bell_draw(arg_keys[8], (LAYERS, D, FF), D ** -0.5, 0.1875, ((0, 2), (1, 8), (2, 8))),
        "w_down": bell_draw(arg_keys[9], (LAYERS, FF, D), FF ** -0.5, 0.09375, ((0, 2), (1, 8), (2, 8))),
    }


highest = lax.Precision.HIGHEST
epsilon = 1e-06

@jax.custom_vjp
def low(v):
    return lax.optimization_barrier(v.astype(jnp.bfloat16)).astype(jnp.float32)

@jax.custom_vjp
def low_back(v):
    return v

def low_keep(v):
    return (low(v), None)

def low_pass(kept, grad):
    return (grad,)

def back_keep(v):
    return (v, None)

def back_low(kept, grad):
    return (low(grad),)
low.defvjp(low_keep, low_pass)
low_back.defvjp(back_keep, back_low)

def sinus_embed(steps_in, width):
    half_width = width // 2
    frequency = jnp.exp(-math.log(10000.0) * jnp.arange(half_width, dtype=jnp.float32) / half_width)
    angles = steps_in.astype(jnp.float32)[:, None] * frequency[None, :]
    return jnp.concatenate([jnp.cos(angles), jnp.sin(angles)], axis=1)

def norm_mod(values, shifts, scales):
    centre = lax.optimization_barrier(jnp.mean(values, axis=-1, keepdims=True))
    centred = values - centre
    spread = lax.optimization_barrier(jnp.mean(centred * centred, axis=-1, keepdims=True))
    return centred * lax.rsqrt(spread + epsilon) * (1.0 + scales) + shifts

def block(tokens, mod_rows, qkv_w, out_w, up_w, down_w):
    seq_len = tokens.shape[0]
    shift_one, scale_one, gate_one, shift_two, scale_two, gate_two = [mod_rows[member] for member in range(6)]
    normed = low(norm_mod(tokens, shift_one, scale_one))
    triple = jnp.einsum('sd,dcn->scn', normed, qkv_w, precision=highest)
    triple = low(low_back(triple))
    queries = triple[:, 0].reshape(seq_len, HEADS, HEAD_DIM)
    keys_all = triple[:, 1].reshape(seq_len, HEADS, HEAD_DIM)
    values_all = triple[:, 2].reshape(seq_len, HEADS, HEAD_DIM)
    scores = jnp.einsum('qhd,khd->hqk', queries, keys_all, precision=highest) * (1.0 / math.sqrt(HEAD_DIM))
    scores = low_back(scores)
    attn_probs = jax.nn.softmax(scores, axis=-1)
    attended = jnp.einsum('hqk,khd->qhd', low(attn_probs), values_all, precision=highest).reshape(seq_len, D)
    attended = low(low_back(attended))
    branch = low_back(jnp.dot(attended, out_w, precision=highest))
    middle = tokens + gate_one * branch
    normed_two = low(norm_mod(middle, shift_two, scale_two))
    pre_act = low_back(jnp.dot(normed_two, up_w, precision=highest))
    hidden = low(jax.nn.gelu(pre_act, approximate=True))
    mlp_out = low_back(jnp.dot(hidden, down_w, precision=highest))
    return middle + gate_two * mlp_out

def reference(latents, cotangent, labels, steps, label_table, w_ada, w_qkv, w_out, w_up, w_down):
    params = tuple((tensor.astype(jnp.float32) for tensor in (latents, label_table, w_ada, w_qkv, w_out, w_up, w_down)))

    def forward(inputs, table, ada_w, qkv_w, out_w, up_w, down_w):
        condition = table[labels] + sinus_embed(steps, D)
        cond_act = low(jax.nn.silu(condition))
        mod_list = []
        for layer_no in range(LAYERS):
            raw_mod = jnp.einsum('ld,dkn->lkn', cond_act, ada_w[layer_no], precision=highest)
            mod_list.append(low(low_back(raw_mod)))
        stacked = jnp.stack(mod_list, axis=1)

        def per_latent(pair_in):
            tokens, mod_rows = pair_in
            for layer_no in range(LAYERS):
                tokens = block(tokens, mod_rows[layer_no], qkv_w[layer_no], out_w[layer_no], up_w[layer_no], down_w[layer_no])
            return tokens
        return lax.map(jax.checkpoint(per_latent), (inputs, stacked))
    result, pullback = jax.vjp(forward, *params)
    gradients = pullback(cotangent.astype(jnp.float32))
    ends = jnp.stack([gradients[0], result], axis=0)
    return (ends, gradients[1], gradients[2], gradients[3], gradients[4], gradients[5], gradients[6])
```

```python
import functools
import math

import jax
import jax.numpy as jnp
from jax import lax
from jax.experimental import pallas as pl
from jax.experimental.pallas import tpu as pltpu
from jax.sharding import PartitionSpec as P


LAT = 3
HEAD = 64
EPS = 1e-06
GELU_C = math.sqrt(2.0 / math.pi)
GELU_A = 0.044715

f32 = jnp.float32
bf16 = jnp.bfloat16


def sds(shape, dtype):
    return jax.ShapeDtypeStruct(shape, dtype)


def call(kernel, outs, *args):
    vmem = pl.BlockSpec(memory_space=pltpu.VMEM)
    return pl.pallas_call(
        kernel,
        out_shape=tuple(sds(*o) for o in outs),
        in_specs=[
            pl.BlockSpec(memory_space=pltpu.SMEM) if a.dtype == jnp.int32 else vmem for a in args
        ],
        out_specs=tuple(vmem for _ in outs),
        compiler_params=pltpu.CompilerParams(vmem_limit_bytes=48 * 1024 * 1024),
    )(*args)


def mm(a, b):
    return lax.dot_general(a, b, (((1,), (0,)), ((), ())), preferred_element_type=f32)


def mm_nt(a, b):
    return lax.dot_general(a, b, (((1,), (1,)), ((), ())), preferred_element_type=f32)


def mm_tn(a, b):
    return lax.dot_general(a, b, (((0,), (0,)), ((), ())), preferred_element_type=f32)


def part(mod, k):
    return jnp.concatenate(
        [jnp.broadcast_to(mod[3 * k + l : 3 * k + l + 1, :], (8, mod.shape[1])) for l in range(LAT)],
        axis=0,
    )


def centred(x):
    c = x - jnp.mean(x, axis=-1, keepdims=True)
    r = lax.rsqrt(jnp.mean(c * c, axis=-1, keepdims=True) + EPS)
    return c * r, r


def norm_back(x, dy, scale):
    xh, r = centred(x)
    g = dy * (1.0 + scale)
    dx = r * (
        g - jnp.mean(g, axis=-1, keepdims=True) - xh * jnp.mean(g * xh, axis=-1, keepdims=True)
    )
    return dx, dy, dy * xh


def row_sums(ref, at, v):
    for l in range(LAT):
        ref[3 * at + l : 3 * at + l + 1, :] = jnp.sum(v[8 * l : 8 * l + 8, :], axis=0, keepdims=True)


def summed(ref, *at):
    total = ref[(0, *at)].astype(f32)
    for j in range(1, 8):
        total = total + ref[(j, *at)].astype(f32)
    return total


def to_all(ref, v):
    for j in range(8):
        ref[j] = v


def by_latent(v):
    v = v.reshape(8, LAT, 8, v.shape[-1])
    return [v[:, l].reshape(64, v.shape[-1]) for l in range(LAT)]


def by_part(vs):
    w = vs[0].shape[-1]
    return jnp.stack([v.reshape(8, 8, w) for v in vs], axis=1).reshape(192, w)


def gelu_parts(x):
    t = jnp.tanh(GELU_C * (x + GELU_A * (x * x * x)))
    return t


def k_norm_first(x_ref, mod_ref, o_ref):
    mod = mod_ref[...].astype(f32)
    shift, scale = part(mod, 0), 1.0 + part(mod, 1)
    for j in range(8):
        xh, _ = centred(x_ref[j])
        o_ref[j] = (xh * scale + shift).astype(bf16)


def k_qkv(n_ref, w_ref, q_ref, kv_ref):
    y = mm(n_ref[...], w_ref[:, :384])
    for l, v in enumerate(by_latent(y)):
        q_ref[l] = v[:, :128].astype(bf16)
        kv_ref[l] = v[:, 128:].astype(bf16)


def head_rows(v):
    lane = lax.broadcasted_iota(jnp.int32, v.shape, 1)
    zero = jnp.zeros_like(v)
    return jnp.concatenate(
        [jnp.where(lane < HEAD, v, zero), jnp.where(lane < HEAD, zero, v)], axis=0
    )


def head_lanes(v):
    lane = lax.broadcasted_iota(jnp.int32, (64, 128), 1)
    return jnp.where(lane < HEAD, v[:64], v[64:])


def keys_values(a_ref, b_ref, l):
    kv = jnp.concatenate([a_ref[c, l] for c in range(8)] + [b_ref[c, l] for c in range(8)], axis=0)
    return kv[:, :128], kv[:, 128:]


def soft(qs, k):
    s = mm_nt(qs, k) * 0.125
    e = jnp.exp(s - jnp.max(s, axis=-1, keepdims=True))
    return e / jnp.sum(e, axis=-1, keepdims=True)


def k_attn(q_ref, a_ref, b_ref, w_ref, att_ref, o_ref):
    outs = []
    for l in range(LAT):
        k, v = keys_values(a_ref, b_ref, l)
        probs = soft(head_rows(q_ref[l].astype(f32)).astype(bf16), k)
        outs.append(head_lanes(mm(probs.astype(bf16), v)))
    att = by_part(outs).astype(bf16)
    att_ref[...] = att
    o_ref[...] = mm_nt(att, w_ref[:, 384:]).astype(bf16)


def k_attn_back(q_ref, a_ref, b_ref, w_ref, db_ref, dq_ref, da_ref, dp_ref):
    datt = by_latent(mm(db_ref[...], w_ref[:, 384:]))
    for l in range(LAT):
        k, v = keys_values(a_ref, b_ref, l)
        qs = head_rows(q_ref[l].astype(f32)).astype(bf16)
        do = head_rows(datt[l]).astype(bf16)
        probs = soft(qs, k)
        dprobs = mm_nt(do, v)
        dv = mm_tn(probs.astype(bf16), do)
        ds = probs * (dprobs - jnp.sum(probs * dprobs, axis=-1, keepdims=True))
        ds = ds.astype(bf16)
        dk = mm_tn(ds, qs) * 0.125
        dq_ref[l] = (head_lanes(mm(ds, k)) * 0.125).astype(bf16)
        dkv = jnp.concatenate([dk, dv], axis=1).astype(bf16)
        for c in range(8):
            da_ref[c, l] = dkv[64 * c : 64 * c + 64]
            dp_ref[c, l] = dkv[512 + 64 * c : 512 + 64 * c + 64]


def k_pair_sum(a_ref, b_ref, o_ref):
    o_ref[...] = (a_ref[...].astype(f32) + b_ref[...].astype(f32)).astype(bf16)


def k_qkv_back(dq_ref, r_ref, w_ref, dt_ref, o_ref):
    rows = []
    for l in range(LAT):
        dkv = summed(r_ref, l)
        rows.append(jnp.concatenate([dq_ref[l].astype(f32), dkv], axis=1))
    dt = by_part(rows).astype(bf16)
    dt_ref[...] = dt
    o_ref[...] = mm_nt(dt, w_ref[:, :384]).astype(bf16)


def k_mid(r_ref, x_ref, mod_ref, br_ref, mid_ref, o_ref):
    mod = mod_ref[...].astype(f32)
    branch = summed(r_ref)
    mid = x_ref[...] + part(mod, 2) * branch
    br_ref[...] = branch
    mid_ref[...] = mid
    xh, _ = centred(mid)
    to_all(o_ref, (xh * (1.0 + part(mod, 4)) + part(mod, 3)).astype(bf16))


def k_mlp(n_ref, w_ref, pre_ref, hid_ref, o_ref):
    pre = mm(n_ref[...], w_ref[:, :512])
    pre_ref[...] = pre
    hid = (0.5 * pre * (1.0 + gelu_parts(pre))).astype(bf16)
    hid_ref[...] = hid
    o_ref[...] = mm_nt(hid, w_ref[:, 512:]).astype(bf16)


def gelu_slope(pre, t):
    inner = GELU_C * (1.0 + 3.0 * GELU_A * pre * pre)
    return 0.5 * (1.0 + t) + 0.5 * pre * (1.0 - t * t) * inner


def k_mlp_both(n_ref, w_ref, dm_ref, hid_ref, dpre_ref, o_ref):
    pre = mm(n_ref[...], w_ref[:, :512])
    t = gelu_parts(pre)
    hid = (0.5 * pre * (1.0 + t)).astype(bf16)
    hid_ref[...] = hid
    out = mm_nt(hid, w_ref[:, 512:]).astype(bf16)
    dhid = mm(dm_ref[...], w_ref[:, 512:])
    dpre = (dhid * gelu_slope(pre, t)).astype(bf16)
    dpre_ref[...] = dpre
    back = mm_nt(dpre, w_ref[:, :512]).astype(bf16)
    for j in range(8):
        o_ref[j, 0] = out[24 * j : 24 * j + 24]
        o_ref[j, 1] = back[24 * j : 24 * j + 24]


def k_mlp_back(pre_ref, w_ref, dm_ref, dpre_ref, o_ref):
    pre = pre_ref[...]
    dhid = mm(dm_ref[...], w_ref[:, 512:])
    dpre = (dhid * gelu_slope(pre, gelu_parts(pre))).astype(bf16)
    dpre_ref[...] = dpre
    o_ref[...] = mm_nt(dpre, w_ref[:, :512]).astype(bf16)


def k_gate_rows(c_ref, mod_ref, o_ref):
    gate = part(mod_ref[...].astype(f32), 5)
    for j in range(8):
        o_ref[j] = (gate * c_ref[j]).astype(bf16)


def k_next(r_ref, mid_ref, mod_ref, mod_next_ref, mlp_ref, x_ref, o_ref):
    mod, mod_next = mod_ref[...].astype(f32), mod_next_ref[...].astype(f32)
    mlp = summed(r_ref)
    mlp_ref[...] = mlp
    x = mid_ref[...] + part(mod, 5) * mlp
    x_ref[...] = x
    xh, _ = centred(x)
    to_all(o_ref, (xh * (1.0 + part(mod_next, 1)) + part(mod_next, 0)).astype(bf16))


def back_two(mod, mid, branch, dy, dn, mlp, dmid_ref, dmod_ref, o_ref):
    dx, ds, dc = norm_back(mid, dn, part(mod, 4))
    dmid = dy + dx
    dmid_ref[...] = dmid
    row_sums(dmod_ref, 0, dmid * branch)
    row_sums(dmod_ref, 1, ds)
    row_sums(dmod_ref, 2, dc)
    row_sums(dmod_ref, 3, dy * mlp)
    to_all(o_ref, (part(mod, 2) * dmid).astype(bf16))


def k_last(r_ref, mid_ref, br_ref, dy_ref, mod_ref, res_ref, dmid_ref, dmod_ref, o_ref):
    mod = mod_ref[...].astype(f32)
    mlp, dn = summed(r_ref, 0), summed(r_ref, 1)
    mid = mid_ref[...]
    res_ref[...] = (mid + part(mod, 5) * mlp).astype(bf16)
    back_two(mod, mid, br_ref[...], dy_ref[...], dn, mlp, dmid_ref, dmod_ref, o_ref)


def k_back_two(r_ref, mid_ref, br_ref, dy_ref, mlp_ref, mod_ref, dmid_ref, dmod_ref, o_ref):
    mod = mod_ref[...].astype(f32)
    back_two(
        mod, mid_ref[...], br_ref[...], dy_ref[...], summed(r_ref), mlp_ref[...],
        dmid_ref, dmod_ref, o_ref,
    )


def k_back_one(r_ref, x_ref, dmid_ref, mod_ref, mod_before_ref, dx_ref, dmod_ref, o_ref):
    dx, ds, dc = norm_back(x_ref[...], summed(r_ref), part(mod_ref[...].astype(f32), 1))
    dx = dmid_ref[...] + dx
    dx_ref[...] = dx
    row_sums(dmod_ref, 0, ds)
    row_sums(dmod_ref, 1, dc)
    to_all(o_ref, (part(mod_before_ref[...].astype(f32), 5) * dx).astype(bf16))


def k_back_first(r_ref, x_ref, dmid_ref, mod_ref, dx_ref, dmod_ref):
    dx, ds, dc = norm_back(x_ref[...], summed(r_ref), part(mod_ref[...].astype(f32), 1))
    dx_ref[...] = (dmid_ref[...] + dx).astype(bf16)
    row_sums(dmod_ref, 0, ds)
    row_sums(dmod_ref, 1, dc)


def k_grad_mlp(p_ref, n_ref, dpre_ref, dm_ref, hid_ref, keep_ref, send_ref):
    def put(up_ref, down_ref):
        up_ref[...] = mm_tn(n_ref[...], dpre_ref[...]).astype(bf16)
        down_ref[...] = mm_tn(dm_ref[...], hid_ref[...]).astype(bf16)

    @pl.when(p_ref[0] == 0)
    def _():
        put(keep_ref, send_ref)

    @pl.when(p_ref[0] == 1)
    def _():
        put(send_ref, keep_ref)


def k_grad_attn(p_ref, n_ref, dt_ref, db_ref, att_ref, keep_ref, send_ref):
    def put(a_ref, b_ref):
        a_ref[...] = mm_tn(n_ref[...], dt_ref[:, :256]).astype(bf16)
        b_ref[:, :128] = mm_tn(n_ref[...], dt_ref[:, 256:]).astype(bf16)
        b_ref[:, 128:] = mm_tn(db_ref[...], att_ref[...]).astype(bf16)

    @pl.when(p_ref[0] == 0)
    def _():
        put(keep_ref, send_ref)

    @pl.when(p_ref[0] == 1)
    def _():
        put(send_ref, keep_ref)


def exchange(x, axis):
    return lax.all_to_all(x, axis, 0, 0, tiled=True)


def swap(x):
    return lax.ppermute(x, "pipe", [(0, 1), (1, 0)])


def copies(x, n):
    return jnp.broadcast_to(x[None], (n, *x.shape))


def body(latents, cotangent, labels, steps, label_table, w_ada, w_qkv, w_out, w_up, w_down):
    p, t = lax.axis_index("pipe"), lax.axis_index("tp")
    first = p == 0
    who = p.astype(jnp.int32).reshape(1)
    width = latents.shape[2]

    def of_layer(own, other):
        return jnp.where(first, own, other), jnp.where(first, other, own)

    w_attn = jnp.concatenate([w_qkv[0].reshape(128, 384), w_out[0].T], axis=1)
    w_mlp = jnp.concatenate([w_up[0], w_down[0].T], axis=1)
    w_mlp = lax.all_gather(w_mlp, "ctx", axis=0, tiled=True)
    w_attn = exchange(copies(w_attn, 8), "ctx").reshape(1024, 512)
    wa = of_layer(w_attn, swap(w_attn))

    rows = [lax.dynamic_slice_in_dim(label_table, labels[l], 1, 0) for l in range(LAT)]
    half = width // 2
    freq = jnp.exp(-math.log(10000.0) * jnp.arange(half, dtype=f32) / half)
    angles = steps.astype(f32)[:, None] * freq[None, :]
    condition = jnp.concatenate(rows, axis=0).astype(f32) + jnp.concatenate(
        [jnp.cos(angles), jnp.sin(angles)], axis=1
    )
    cond_act = jax.nn.silu(condition).astype(bf16)
    ada = w_ada[0].transpose(1, 2, 0)
    mod_piece = jnp.einsum("ld,knd->kln", cond_act, ada, preferred_element_type=f32)
    mod_piece = mod_piece.astype(bf16).reshape(18, 16)
    placed = lax.dynamic_update_slice(jnp.zeros((18, 128), bf16), mod_piece, (0, 16 * t))
    placed = exchange(copies(placed, 64), ("ctx", "tp")).reshape(8, 8, 18, 128)
    mod_own = placed.astype(f32).sum(axis=1).transpose(1, 0, 2).reshape(18, 1024).astype(bf16)
    mods = of_layer(mod_own, swap(mod_own))

    def own_rows(a):
        a = lax.dynamic_slice_in_dim(a, 64 * p, 64, 1)
        a = a.reshape(LAT, 8, 8, width).transpose(1, 0, 2, 3).reshape(8, 24, width)
        return a, lax.dynamic_index_in_dim(a, t, 0, keepdims=False)

    x_all, x0 = own_rows(latents)
    cot_all, cot = own_rows(cotangent)

    bc = ((8, 24, 1024), bf16)
    rows24 = ((24, 1024), f32)
    wide = ((192, 1024), bf16)
    kv_shape = ((8, LAT, 64, 256), bf16)

    def attn_forward(normed, w):
        q, kv = call(k_qkv, [((LAT, 64, 128), bf16), ((LAT, 64, 256), bf16)], normed, w)
        kv_a = exchange(copies(kv, 8), "ctx")
        kv_b = swap(kv_a)
        att, branch = call(k_attn, [((192, 128), bf16), wide], q, kv_a, kv_b, w)
        return (q, kv_a, kv_b, att), exchange(branch.reshape(8, 24, 1024), "tp")

    def attn_back(kept, normed, dbranch, w):
        q, kv_a, kv_b, att = kept
        dq, da, dp = call(
            k_attn_back, [((LAT, 64, 128), bf16), kv_shape, kv_shape], q, kv_a, kv_b, w, dbranch
        )
        (both,) = call(k_pair_sum, [kv_shape], da, swap(dp))
        arrived = exchange(both, "ctx")
        dt, dn = call(k_qkv_back, [((192, 384), bf16), wide], dq, arrived, w)
        halves = call(
            k_grad_attn, [((1024, 256), bf16)] * 2, who, normed, dt, dbranch, att
        )
        return exchange(dn.reshape(8, 24, 1024), "tp"), halves

    def grads_mlp(n, dpre, dm, hid):
        return call(k_grad_mlp, [((1024, 512), bf16)] * 2, who, n, dpre, dm, hid)

    def to_rows(x):
        return exchange(x, "tp").reshape(192, 1024)

    (normed0,) = call(k_norm_first, [bc], x_all, mods[0])
    normed0 = normed0.reshape(192, 1024)
    kept0, arrived = attn_forward(normed0, wa[0])
    br0, mid0, n2 = call(k_mid, [rows24, rows24, bc], arrived, x0, mods[0])
    n2_0 = to_rows(n2)
    wm = of_layer(w_mlp, swap(w_mlp))
    pre0, hid0, out = call(
        k_mlp, [((192, 512), f32), ((192, 512), bf16), wide], n2_0, wm[0]
    )
    arrived = exchange(out.reshape(8, 24, 1024), "tp")
    mlp0, x1, n1 = call(k_next, [rows24, rows24, bc], arrived, mid0, mods[0], mods[1])

    normed1 = to_rows(n1)
    kept1, arrived = attn_forward(normed1, wa[1])
    br1, mid1, n2 = call(k_mid, [rows24, rows24, bc], arrived, x1, mods[1])
    n2_1 = to_rows(n2)
    (dm1,) = call(k_gate_rows, [bc], cot_all, mods[1])
    dm1 = dm1.reshape(192, 1024)
    hid1, dpre1, both = call(
        k_mlp_both,
        [((192, 512), bf16), ((192, 512), bf16), ((8, 2, 24, 1024), bf16)],
        n2_1, wm[1], dm1,
    )
    arrived = exchange(both, "tp")
    res1, dmid1, dmod1a, db = call(
        k_last,
        [((24, 1024), bf16), rows24, ((12, 1024), f32), bc],
        arrived, mid1, br1, cot, mods[1],
    )
    keep, send = grads_mlp(n2_1, dpre1, dm1, hid1)
    gm1 = lax.psum_scatter(call(k_pair_sum, [((1024, 512), bf16)], keep, swap(send))[0], "ctx", tiled=True)

    db1 = to_rows(db)
    arrived, halves1 = attn_back(kept1, normed1, db1, wa[1])
    dx1, dmod1b, dm = call(
        k_back_one, [rows24, ((6, 1024), f32), bc], arrived, x1, dmid1, mods[1], mods[0]
    )
    dm0 = to_rows(dm)

    dpre0, dn = call(k_mlp_back, [((192, 512), bf16), wide], pre0, wm[0], dm0)
    arrived = exchange(dn.reshape(8, 24, 1024), "tp")
    dmid0, dmod0a, db = call(
        k_back_two, [rows24, ((12, 1024), f32), bc], arrived, mid0, br0, dx1, mlp0, mods[0]
    )
    keep, send = grads_mlp(n2_0, dpre0, dm0, hid0)
    gm0 = call(k_pair_sum, [((1024, 512), bf16)], keep, swap(send))[0]
    ga1 = call(k_pair_sum, [((1024, 256), bf16)], halves1[0], swap(halves1[1]))[0]
    mixed = lax.psum_scatter(jnp.concatenate([gm0, ga1], axis=1), "ctx", tiled=True)
    gm0, ga1 = mixed[:, :512], mixed[:, 512:]

    db0 = to_rows(db)
    arrived, halves0 = attn_back(kept0, normed0, db0, wa[0])
    dx0, dmod0b = call(
        k_back_first, [((24, 1024), bf16), ((6, 1024), f32)], arrived, x0, dmid0, mods[0]
    )

    def stacked(a, b):
        return jnp.concatenate([b, a], axis=0)

    dmod_own, dmod_other = of_layer(stacked(dmod0a, dmod0b), stacked(dmod1a, dmod1b))
    dmod = (dmod_own + swap(dmod_other)).astype(bf16)
    dmod = dmod.reshape(18, 8, 128).transpose(1, 0, 2)
    dmod = jnp.broadcast_to(dmod[:, None], (8, 8, 18, 128)).reshape(64, 18, 128)
    dmod = exchange(dmod, ("ctx", "tp")).astype(f32).sum(axis=0)
    dmod = lax.dynamic_slice_in_dim(dmod, 16 * t, 16, 1).astype(bf16).reshape(6, 3, 16)
    grad_ada = jnp.einsum("kln,ld->knd", dmod, cond_act, preferred_element_type=f32)
    cond_part = jnp.einsum("kln,knd->ld", dmod, ada, preferred_element_type=f32)
    cond_part = (cond_part + swap(cond_part)).reshape(24, 128)
    grad_act = exchange(copies(cond_part, 64), ("ctx", "tp")).sum(axis=0).reshape(LAT, width)
    sig = jax.nn.sigmoid(condition)
    grad_cond = grad_act * (sig * (1.0 + condition * (1.0 - sig)))
    classes = jnp.arange(label_table.shape[0], dtype=jnp.int32)[:, None]
    grad_table = sum(
        jnp.where(classes == labels[l], grad_cond[l : l + 1], 0.0) for l in range(LAT)
    )

    ga0 = call(k_pair_sum, [((1024, 256), bf16)], halves0[0], swap(halves0[1]))[0]
    ga0 = exchange(ga0.reshape(8, 128, 256), "ctx").astype(f32).sum(axis=0).astype(bf16)

    mine = jnp.concatenate([jnp.where(first, gm0, gm1), jnp.where(first, ga0, ga1)], axis=1)
    send = jnp.concatenate([jnp.where(first, gm1, gm0), jnp.where(first, ga1, ga0)], axis=1)
    half0, half1 = of_layer(mine, swap(send))
    grad_up = half0[:, :512].astype(f32)
    grad_down = half1[:, :512].astype(f32).T
    grad_qkv = jnp.concatenate([half0[:, 512:], half1[:, 512:640]], axis=1).astype(f32)
    grad_out = half1[:, 640:].astype(f32).T

    mine = jnp.where(first, dx0, res1)
    other = swap(jnp.where(first, res1, dx0))
    pair = jnp.stack(of_layer(mine, other))
    ends = exchange(copies(pair, 8), "tp").reshape(8, 2, LAT, 8, width)
    ends = ends.transpose(2, 1, 0, 3, 4).reshape(LAT, 128, width).astype(f32)

    return (
        ends[None],
        grad_table,
        grad_ada.transpose(2, 0, 1)[None],
        grad_qkv.reshape(1, 128, 3, 128),
        grad_out[None],
        grad_up[None],
        grad_down[None],
    )


def solution(mesh):
    return jax.shard_map(
        body,
        mesh=mesh,
        in_specs=(
            P(None, "ctx", None),
            P(None, "ctx", None),
            P(),
            P(),
            P(),
            P("pipe", None, None, ("ctx", "tp")),
            P("pipe", "ctx", None, "tp"),
            P("pipe", "tp", "ctx"),
            P("pipe", "ctx", "tp"),
            P("pipe", "tp", "ctx"),
        ),
        out_specs=(
            P("pipe", None, "ctx", None),
            P(),
            P("pipe", None, None, ("ctx", "tp")),
            P("pipe", "ctx", None, "tp"),
            P("pipe", "tp", "ctx"),
            P("pipe", "ctx", "tp"),
            P("pipe", "tp", "ctx"),
        ),
        check_vma=False,
    )
```

```python
import math

import jax
import jax.numpy as jnp
from jax import lax
from jax.experimental import pallas as pl
from jax.experimental.pallas import tpu as pltpu
from jax.sharding import PartitionSpec as P


LAT = 3
HEAD = 64
EPS = 1e-06
GELU_C = math.sqrt(2.0 / math.pi)
GELU_A = 0.044715
STORE_ROWS = 34048

f32 = jnp.float32
bf16 = jnp.bfloat16


def sds(shape, dtype):
    return jax.ShapeDtypeStruct(shape, dtype)


def up16(n):
    return -(-n // 16) * 16


class Slot:
    def __init__(self, row, shape, dtype):
        self.row, self.shape, self.dtype = row, shape, dtype
        self.rows = up16(shape[0]) * (2 if dtype == f32 else 1)

    def of(self, ref):
        return ref.at[pl.ds(self.row, self.rows), pl.ds(0, self.shape[1])]


class Store:
    def __init__(self):
        self.array, self.next = None, 0

    def slot(self, shape, dtype):
        s = Slot(self.next, shape, dtype)
        self.next += s.rows
        assert self.next <= STORE_ROWS
        return s


class Save:
    def __init__(self, array, slot):
        self.array, self.slot = array, slot


class Near:
    def __init__(self, array):
        self.array = array


class Half:
    def __init__(self, core, own, other, block, rows, at, width, slot):
        self.core, self.own, self.other = core, own, other
        self.block, self.rows, self.at, self.width, self.slot = block, rows, at, width, slot


class Held:
    def __init__(self, ref, wait, shape, dtype):
        self.ref, self.wait, self.shape, self.dtype = ref, wait, shape, dtype

    def ready(self):
        if self.wait is not None:
            self.wait()
            self.wait = None

    def __getitem__(self, at):
        self.ready()
        if self.dtype != f32 or self.ref.dtype == f32:
            return self.ref[at]
        n = self.shape[0]
        low = up16(n)
        return self.ref[:n].astype(f32) + self.ref[low : low + n].astype(f32)


class Kept:
    def __init__(self, ref, copy, shape, dtype):
        self.ref, self.copy, self.shape, self.dtype, self.gone = ref, copy, shape, dtype, False

    def send(self):
        if not self.gone:
            self.copy.start()
            self.gone = True

    def __setitem__(self, at, v):
        if self.dtype == f32:
            n = self.shape[0]
            low = up16(n)
            high = v.astype(bf16)
            self.ref[:n] = high
            self.ref[low : low + n] = (v - high.astype(f32)).astype(bf16)
            self.send()
        else:
            self.ref[at] = v
            if at is Ellipsis:
                self.send()


def ready(*refs):
    for r in refs:
        if isinstance(r, Held):
            r.ready()


def call(store, kernel, outs, *args):
    vmem = pl.BlockSpec(memory_space=pltpu.VMEM)
    smem = pl.BlockSpec(memory_space=pltpu.SMEM)
    far = pl.BlockSpec(memory_space=pltpu.HBM)
    uses = any(isinstance(a, (Slot, Save, Half)) for a in args) or any(
        isinstance(o, Slot) for o in outs
    )
    flat, in_specs, plan, scratch = [], [], [], []

    def hold(shape, dtype):
        scratch.append(pltpu.VMEM(shape, dtype))
        return len(scratch) - 1

    for a in args:
        if isinstance(a, Slot):
            plan.append(("slot", a, hold((a.rows, a.shape[1]), bf16)))
        elif isinstance(a, Near):
            plan.append(("near", len(flat), hold(a.array.shape, a.array.dtype)))
            flat.append(a.array)
            in_specs.append(far)
        elif isinstance(a, Half):
            plan.append(("half", len(flat), hold(a.slot.shape, bf16), a))
            flat += [a.own, a.other]
            in_specs += [far, far]
        else:
            v = a.array if isinstance(a, Save) else a
            plan.append(("here", len(flat), a))
            flat.append(v)
            in_specs.append(smem if v.dtype == jnp.int32 else vmem)
    out_shape, out_specs, out_plan = [], [], []
    for o in outs:
        if isinstance(o, Slot):
            out_plan.append((o, hold((o.rows, o.shape[1]), bf16)))
        else:
            out_plan.append((None, len(out_shape)))
            out_shape.append(sds(*o))
            out_specs.append(vmem)
    n_args, n_out, n_hold = len(flat), len(out_shape), len(scratch)
    n_saves = sum(isinstance(a, (Save, Half)) for a in args)
    alias = {}
    if uses:
        if store.array is not None:
            flat.append(store.array)
            in_specs.append(far)
            alias = {len(flat) - 1: n_out}
        out_shape.append(sds((STORE_ROWS, 1024), bf16))
        out_specs.append(far)
    n_in = len(flat)
    n_sems = n_hold + n_saves

    def wrapped(*refs):
        ins, results = refs[:n_in], refs[n_in : n_in + len(out_shape)]
        holds = refs[n_in + len(out_shape) :]
        sems = holds[n_hold] if n_sems else None
        big = results[n_out] if uses else None
        given, leaving, late = [], [], n_hold
        for item in plan:
            if item[0] == "here":
                given.append(ins[item[1]])
                if isinstance(item[2], Save):
                    copy = pltpu.make_async_copy(ins[item[1]], item[2].slot.of(big), sems.at[late])
                    copy.start()
                    leaving.append(copy)
                    late += 1
                continue
            to, sem = holds[item[2]], sems.at[item[2]]
            if item[0] == "half":
                h = item[3]
                mine = lax.axis_index("pipe") == h.core
                for k in range(2):

                    @pl.when(mine if k == 0 else jnp.logical_not(mine))
                    def _(src=ins[item[1] + k]):
                        for c in range(h.slot.shape[0] // h.rows):
                            pltpu.make_async_copy(
                                src.at[pl.ds(c * h.block, h.rows), pl.ds(h.at, h.width)],
                                to.at[pl.ds(c * h.rows, h.rows)],
                                sem,
                            ).start()

                whole = pltpu.make_async_copy(to, to, sem)
                out = pltpu.make_async_copy(to, h.slot.of(big), sems.at[late])
                late += 1
                leaving.append(out)

                def arrive(whole=whole, out=out):
                    whole.wait()
                    out.start()

                given.append(Held(to, arrive, h.slot.shape, bf16))
                continue
            if item[0] == "slot":
                copy = pltpu.make_async_copy(item[1].of(big), to, sem)
                shape, dtype = item[1].shape, item[1].dtype
            else:
                copy = pltpu.make_async_copy(ins[item[1]], to, sem)
                shape, dtype = to.shape, to.dtype
            copy.start()
            given.append(Held(to, copy.wait, shape, dtype))
        for slot, at in out_plan:
            if slot is None:
                given.append(results[at])
            else:
                copy = pltpu.make_async_copy(holds[at], slot.of(big), sems.at[at])
                kept = Kept(holds[at], copy, slot.shape, slot.dtype)
                leaving.append(copy)
                given.append(kept)
        kernel(*given)
        ready(*given)
        for g in given:
            if isinstance(g, Kept):
                g.send()
        for copy in leaving:
            copy.wait()

    got = pl.pallas_call(
        wrapped,
        out_shape=tuple(out_shape),
        in_specs=in_specs,
        out_specs=tuple(out_specs),
        scratch_shapes=scratch + ([pltpu.SemaphoreType.DMA((n_sems,))] if n_sems else []),
        input_output_aliases=alias,
        compiler_params=pltpu.CompilerParams(vmem_limit_bytes=24 * 1024 * 1024),
    )(*flat)
    if uses:
        store.array = got[n_out]
    return got[:n_out]


def mm(a, b):
    return lax.dot_general(a, b, (((1,), (0,)), ((), ())), preferred_element_type=f32)


def mm_nt(a, b):
    return lax.dot_general(a, b, (((1,), (1,)), ((), ())), preferred_element_type=f32)


def mm_tn(a, b):
    return lax.dot_general(a, b, (((0,), (0,)), ((), ())), preferred_element_type=f32)


def part(mod, k):
    return jnp.concatenate(
        [jnp.broadcast_to(mod[3 * k + l : 3 * k + l + 1, :], (8, mod.shape[1])) for l in range(LAT)],
        axis=0,
    )


def centred(x):
    c = x - jnp.mean(x, axis=-1, keepdims=True)
    r = lax.rsqrt(jnp.mean(c * c, axis=-1, keepdims=True) + EPS)
    return c * r, r


def norm_back(x, dy, scale):
    xh, r = centred(x)
    g = dy * (1.0 + scale)
    dx = r * (
        g - jnp.mean(g, axis=-1, keepdims=True) - xh * jnp.mean(g * xh, axis=-1, keepdims=True)
    )
    return dx, dy, dy * xh


def row_sums(*vs):
    return jnp.concatenate(
        [jnp.sum(v[8 * l : 8 * l + 8], axis=0, keepdims=True) for v in vs for l in range(LAT)], axis=0
    )


def summed(ref, *at):
    total = ref[(0, *at)].astype(f32)
    for j in range(1, 8):
        total = total + ref[(j, *at)].astype(f32)
    return total


def to_all(ref, v):
    for j in range(8):
        ref[j] = v


def by_latent(v):
    v = v.reshape(8, LAT, 8, v.shape[-1])
    return [v[:, l].reshape(64, v.shape[-1]) for l in range(LAT)]


def rows_of(v):
    return v.reshape(-1, v.shape[-1])


def by_part(vs):
    w = vs[0].shape[-1]
    return jnp.stack([v.reshape(8, 8, w) for v in vs], axis=1).reshape(192, w)


def gelu_parts(x):
    t = jnp.tanh(GELU_C * (x + GELU_A * (x * x * x)))
    return t


def k_halves(p_ref, wq_ref, wo_ref, up_ref, down_ref, keep_ref, send_ref):
    ready(wq_ref, wo_ref, up_ref, down_ref)

    def put(a_ref, b_ref):
        for k in range(2):
            a_ref[:, 128 * k : 128 * k + 128] = wq_ref[k]
        a_ref[:, 256:] = up_ref[...]
        b_ref[:, :128] = wq_ref[2]
        b_ref[:, 128:256] = wo_ref[...].astype(f32).T.astype(bf16)
        b_ref[:, 256:] = down_ref[...].astype(f32).T.astype(bf16)

    @pl.when(p_ref[0] == 0)
    def _():
        put(keep_ref, send_ref)

    @pl.when(p_ref[0] == 1)
    def _():
        put(send_ref, keep_ref)


def k_pack(
    p_ref, t_ref, lab_ref, table_ref, sinus_ref, ada_ref, keep_ref, got_ref,
    o_ref, w0_ref, w1_ref, cond_ref, act_ref,
):
    first = p_ref[0] == 0
    keep, got = keep_ref[...].astype(f32), got_ref[...].astype(f32)
    w0 = jnp.where(first, keep, got).astype(bf16)
    w0_ref[...] = w0[:, 256:]
    w1_ref[...] = jnp.where(first, got, keep).astype(bf16)
    row = lax.broadcasted_iota(jnp.int32, (8, table_ref.shape[0]), 0)
    col = lax.broadcasted_iota(jnp.int32, (8, table_ref.shape[0]), 1)
    label = jnp.where(row == 0, lab_ref[0], jnp.where(row == 1, lab_ref[1], lab_ref[2]))
    cond = mm(jnp.where(col == label, 1.0, 0.0).astype(bf16), table_ref[...])[:LAT] + sinus_ref[...]
    cond_ref[...] = cond
    act = (cond / (1.0 + jnp.exp(-cond))).astype(bf16)
    act_ref[...] = act
    lane = lax.broadcasted_iota(jnp.int32, (16, 256), 1)
    row = lax.broadcasted_iota(jnp.int32, (16, 256), 0)
    place = jnp.where(lane == row + 16 * t_ref[0], 1.0, 0.0).astype(bf16)
    mod = [mm(mm_nt(act, ada_ref[16 * k : 16 * k + 16]).astype(bf16), place) for k in range(6)]
    mod = jnp.concatenate(mod + [jnp.zeros((14, 256), f32)], axis=0).astype(bf16)
    for j in range(8):
        o_ref[j, :128] = w0[:, :256]
        o_ref[j, 128:] = mod


def k_spread(r_ref, o_ref):
    for c in range(8):
        v = r_ref[c, 128:, :128]
        for j in range(8):
            o_ref[j, c] = v


def k_mods(r_ref, o_ref):
    for c in range(8):
        o_ref[:, 128 * c : 128 * c + 128] = summed(r_ref, c).astype(bf16)


def k_two_layers(p_ref, own_ref, other_ref, a_ref, b_ref):
    own, other, first = own_ref[...].astype(f32), other_ref[...].astype(f32), p_ref[0] == 0
    a_ref[...] = jnp.where(first, own, other).astype(bf16)
    b_ref[...] = jnp.where(first, other, own).astype(bf16)


def put_qkv(y, q_ref, kv_ref):
    y = jnp.concatenate(by_latent(y), axis=0).astype(bf16)
    q_ref[...] = y[:, :128]
    to_all(kv_ref, y[:, 128:])


def triple(n, wa_ref, wb_ref):
    a = mm(n, rows_of(wa_ref[...]))
    return jnp.concatenate([a, mm(n, rows_of(wb_ref[...])[:, :128])], axis=1)


def own_blocks(p_ref, t_ref, x_ref, own_ref):
    start = pl.multiple_of(64 * p_ref[0], 64)
    few = pl.multiple_of(64 * p_ref[0] + 8 * t_ref[0], 8)
    own_ref[...] = jnp.concatenate([x_ref[l, pl.ds(few, 8), :] for l in range(LAT)], axis=0)
    blocks = [x_ref[l, pl.ds(start, 64), :] for l in range(LAT)]
    return [
        jnp.concatenate([b[8 * j : 8 * j + 8] for b in blocks], axis=0) for j in range(8)
    ]


def k_first(p_ref, t_ref, x_ref, mod_ref, wa_ref, wb_ref, own_ref, n_ref, q_ref, kv_ref):
    mod = mod_ref[...].astype(f32)
    shift, scale = part(mod, 0), 1.0 + part(mod, 1)
    x_ref.ready()
    rows = [centred(x)[0] * scale + shift for x in own_blocks(p_ref, t_ref, x_ref.ref, own_ref)]
    n = jnp.concatenate(rows, axis=0).astype(bf16)
    n_ref[...] = n
    put_qkv(triple(n, wa_ref, wb_ref), q_ref, kv_ref)


def k_qkv(n_ref, wa_ref, wb_ref, q_ref, kv_ref):
    put_qkv(triple(n_ref[...], wa_ref, wb_ref), q_ref, kv_ref)


def head_rows(v):
    lane = lax.broadcasted_iota(jnp.int32, v.shape, 1)
    zero = jnp.zeros_like(v)
    return jnp.concatenate(
        [jnp.where(lane < HEAD, v, zero), jnp.where(lane < HEAD, zero, v)], axis=0
    )


def head_lanes(v):
    lane = lax.broadcasted_iota(jnp.int32, (64, 128), 1)
    return jnp.where(lane < HEAD, v[:64], v[64:])


def keys_values(a_ref, b_ref, l):
    at = [64 * (LAT * c + l) for c in range(8)]
    kv = jnp.concatenate([r[i : i + 64] for r in (a_ref, b_ref) for i in at], axis=0)
    return kv[:, :128], kv[:, 128:]


def soft(qs, k):
    s = mm_nt(qs, k) * 0.125
    e = jnp.exp(s - jnp.max(s, axis=-1, keepdims=True))
    return e / jnp.sum(e, axis=-1, keepdims=True)


def k_attn(q_ref, a_ref, b_ref, w_ref, att_ref, o_ref):
    outs = []
    for l in range(LAT):
        k, v = keys_values(a_ref, b_ref, l)
        probs = soft(head_rows(q_ref[64 * l : 64 * l + 64].astype(f32)).astype(bf16), k)
        outs.append(head_lanes(mm(probs.astype(bf16), v)))
    att = by_part(outs).astype(bf16)
    att_ref[...] = att
    o_ref[...] = mm_nt(att, rows_of(w_ref[...])[:, 128:]).astype(bf16)


def k_attn_back(q_ref, a_ref, b_ref, w_ref, db_ref, dq_ref, da_ref, dp_ref):
    datt = by_latent(mm(db_ref[...], rows_of(w_ref[...])[:, 128:]))
    for l in range(LAT):
        k, v = keys_values(a_ref, b_ref, l)
        qs = head_rows(q_ref[64 * l : 64 * l + 64].astype(f32)).astype(bf16)
        do = head_rows(datt[l]).astype(bf16)
        probs = soft(qs, k)
        dprobs = mm_nt(do, v)
        dv = mm_tn(probs.astype(bf16), do)
        ds = probs * (dprobs - jnp.sum(probs * dprobs, axis=-1, keepdims=True))
        ds = ds.astype(bf16)
        dk = mm_tn(ds, qs) * 0.125
        dq_ref[64 * l : 64 * l + 64] = (head_lanes(mm(ds, k)) * 0.125).astype(bf16)
        dkv = jnp.concatenate([dk, dv], axis=1).astype(bf16)
        for c in range(8):
            at = 64 * (LAT * c + l)
            da_ref[at : at + 64] = dkv[64 * c : 64 * c + 64]
            dp_ref[at : at + 64] = dkv[512 + 64 * c : 512 + 64 * c + 64]


def k_pair_sum(a_ref, b_ref, o_ref):
    o_ref[...] = (a_ref[...].astype(f32) + b_ref[...].astype(f32)).astype(bf16)


def k_qkv_back(dq_ref, r_ref, wa_ref, wb_ref, dt_ref, o_ref):
    dt = jnp.concatenate([dq_ref[...].astype(f32), summed(r_ref)], axis=1)
    dt = by_part([dt[64 * l : 64 * l + 64] for l in range(LAT)]).astype(bf16)
    dt_ref[...] = dt
    back = mm_nt(dt[:, :256], rows_of(wa_ref[...])) + mm_nt(dt[:, 256:], rows_of(wb_ref[...])[:, :128])
    o_ref[...] = back.astype(bf16)


def k_mid(r_ref, x_ref, mod_ref, br_ref, mid_ref, o_ref):
    mod = mod_ref[...].astype(f32)
    branch = summed(r_ref)
    mid = x_ref[...] + part(mod, 2) * branch
    br_ref[...] = branch
    mid_ref[...] = mid
    xh, _ = centred(mid)
    to_all(o_ref, (xh * (1.0 + part(mod, 4)) + part(mod, 3)).astype(bf16))


def k_mlp(n_ref, up_ref, down_ref, hid_ref, o_ref):
    pre = mm(n_ref[...], rows_of(up_ref[...]))
    hid = (0.5 * pre * (1.0 + gelu_parts(pre))).astype(bf16)
    hid_ref[...] = hid
    o_ref[...] = mm_nt(hid, rows_of(down_ref[...])).astype(bf16)


def gelu_slope(pre, t):
    inner = GELU_C * (1.0 + 3.0 * GELU_A * pre * pre)
    return 0.5 * (1.0 + t) + 0.5 * pre * (1.0 - t * t) * inner


def k_mlp_both(n_ref, up_ref, down_ref, dm_ref, hid_ref, dpre_ref, o_ref):
    pre = mm(n_ref[...], rows_of(up_ref[...]))
    t = gelu_parts(pre)
    hid = (0.5 * pre * (1.0 + t)).astype(bf16)
    hid_ref[...] = hid
    out = mm_nt(hid, rows_of(down_ref[...])).astype(bf16)
    dhid = mm(dm_ref[...], rows_of(down_ref[...]))
    dpre = (dhid * gelu_slope(pre, t)).astype(bf16)
    dpre_ref[...] = dpre
    back = mm_nt(dpre, rows_of(up_ref[...])).astype(bf16)
    for j in range(8):
        o_ref[j, 0] = out[24 * j : 24 * j + 24]
        o_ref[j, 1] = back[24 * j : 24 * j + 24]


def k_mlp_back(n_ref, up_ref, down_ref, dm_ref, dpre_ref, o_ref):
    pre = mm(n_ref[...], rows_of(up_ref[...]))
    dhid = mm(dm_ref[...], rows_of(down_ref[...]))
    dpre = (dhid * gelu_slope(pre, gelu_parts(pre))).astype(bf16)
    dpre_ref[...] = dpre
    o_ref[...] = mm_nt(dpre, rows_of(up_ref[...])).astype(bf16)


def k_gate_rows(p_ref, t_ref, c_ref, mod_ref, own_ref, o_ref):
    gate = part(mod_ref[...].astype(f32), 5)
    c_ref.ready()
    rows = [gate * c for c in own_blocks(p_ref, t_ref, c_ref.ref, own_ref)]
    o_ref[...] = jnp.concatenate(rows, axis=0).astype(bf16)


def k_next(r_ref, mid_ref, mod_ref, mod_next_ref, mlp_ref, x_ref, o_ref):
    mod, mod_next = mod_ref[...].astype(f32), mod_next_ref[...].astype(f32)
    mlp = summed(r_ref)
    mlp_ref[...] = mlp
    x = mid_ref[...] + part(mod, 5) * mlp
    x_ref[...] = x
    xh, _ = centred(x)
    to_all(o_ref, (xh * (1.0 + part(mod_next, 1)) + part(mod_next, 0)).astype(bf16))


def back_two(mod, mid, branch, dy, dn, mlp, dmid_ref, dmod_ref, o_ref):
    dx, ds, dc = norm_back(mid, dn, part(mod, 4))
    dmid = dy + dx
    dmid_ref[...] = dmid
    to_all(o_ref, (part(mod, 2) * dmid).astype(bf16))
    dmod_ref[...] = row_sums(dmid * branch, ds, dc, dy * mlp)


def k_last(r_ref, mid_ref, br_ref, dy_ref, mod_ref, res_ref, dmid_ref, dmod_ref, o_ref):
    mod = mod_ref[...].astype(f32)
    mlp, dn = summed(r_ref, 0), summed(r_ref, 1)
    mid = mid_ref[...]
    res_ref[...] = mid + part(mod, 5) * mlp
    back_two(mod, mid, br_ref[...], dy_ref[...], dn, mlp, dmid_ref, dmod_ref, o_ref)


def k_back_two(r_ref, mid_ref, br_ref, dy_ref, mlp_ref, mod_ref, dmid_ref, dmod_ref, o_ref):
    mod = mod_ref[...].astype(f32)
    back_two(
        mod, mid_ref[...], br_ref[...], dy_ref[...], summed(r_ref), mlp_ref[...],
        dmid_ref, dmod_ref, o_ref,
    )


def k_back_one(r_ref, x_ref, dmid_ref, mod_ref, mod_before_ref, dx_ref, dmod_ref, o_ref):
    dx, ds, dc = norm_back(x_ref[...], summed(r_ref), part(mod_ref[...].astype(f32), 1))
    dx = dmid_ref[...] + dx
    dx_ref[...] = dx
    dmod_ref[...] = row_sums(ds, dc)
    to_all(o_ref, (part(mod_before_ref[...].astype(f32), 5) * dx).astype(bf16))


def k_back_first(
    p_ref, r_ref, x_ref, dmid_ref, mod_ref, d0_ref, d1a_ref, d1b_ref, res_ref, keep_ref, send_ref
):
    first = p_ref[0] == 0
    dx, ds, dc = norm_back(x_ref[...], summed(r_ref), part(mod_ref[...].astype(f32), 1))
    dx = dmid_ref[...] + dx
    res = res_ref[...]
    keep_ref[:24] = jnp.where(first, dx, res)
    send_ref[:24] = jnp.where(first, res, dx)
    none = jnp.zeros((6, dx.shape[1]), f32)
    d0 = jnp.concatenate([row_sums(ds, dc), d0_ref[...], none], axis=0)
    d1 = jnp.concatenate([d1b_ref[...], d1a_ref[...], none], axis=0)
    keep_ref[24:] = jnp.where(first, d0, d1)
    send_ref[24:] = jnp.where(first, d1, d0)


def k_tail_tp(p_ref, keep_ref, got_ref, o_ref):
    first = p_ref[0] == 0
    keep, got = keep_ref[...], got_ref[...]
    v = jnp.concatenate(
        [
            jnp.where(first, keep[:24], got[:24]),
            jnp.where(first, got[:24], keep[:24]),
            keep[24:] + got[24:],
        ],
        axis=0,
    ).astype(bf16)
    to_all(o_ref, v)


def k_tail_ctx(r_ref, a_ref, b_ref, o_ref):
    total = r_ref[0].astype(f32)[48:]
    for j in range(1, 8):
        total = total + r_ref[j].astype(f32)[48:]
    total = jnp.concatenate([total, jnp.zeros((8, total.shape[1]), f32)], axis=0).astype(bf16)
    both = (a_ref[...].astype(f32) + b_ref[...].astype(f32)).astype(bf16)
    none = jnp.zeros((32, 128), bf16)
    for c in range(8):
        o_ref[c, :128, :] = both[128 * c : 128 * c + 128]
        o_ref[c, 128:, :128] = total[:, 128 * c : 128 * c + 128]
        o_ref[c, 128:, 128:] = none


def k_ends(r_ref, o_ref):
    for j in range(8):
        v = r_ref[j].astype(f32)
        for half in range(2):
            for l in range(LAT):
                at = 64 * half + 8 * j
                o_ref[l, at : at + 8, :] = v[24 * half + 8 * l : 24 * half + 8 * l + 8]


def k_cond(t_ref, r_ref, act_ref, ada_ref, g_ref, ada_grad_ref, c_ref):
    total = summed(r_ref)
    g_ref[...] = total[:128].astype(bf16)
    d = total[128:, :128].astype(bf16)
    lane = lax.broadcasted_iota(jnp.int32, (128, 16), 0)
    col = lax.broadcasted_iota(jnp.int32, (128, 16), 1)
    pick = jnp.where(lane == col + 16 * t_ref[0], 1.0, 0.0).astype(bf16)
    d = mm(d, pick)
    act = act_ref[...]
    c = jnp.zeros(c_ref.shape, f32)
    for k in range(6):
        dk = d[3 * k : 3 * k + 3].astype(bf16)
        ada_grad_ref[16 * k : 16 * k + 16, :] = mm_tn(dk, act)
        c = c + mm(dk, ada_ref[16 * k : 16 * k + 16, :])
    c_ref[...] = c


def k_grad_mlp(p_ref, n_ref, dpre_ref, dm_ref, hid_ref, keep_ref, send_ref):
    first = p_ref[0] == 0
    n, dm = n_ref[...], dm_ref[...]
    dpre, hid = dpre_ref[...], hid_ref[...]

    def pick(a, b):
        return jnp.where(first, a.astype(f32), b.astype(f32)).astype(bf16)

    send_ref[...] = mm_tn(pick(dm, n), pick(hid, dpre)).astype(bf16)
    keep_ref[...] = mm_tn(pick(n, dm), pick(dpre, hid)).astype(bf16)


def k_grad_attn(p_ref, n_ref, dt_ref, db_ref, att_ref, keep_ref, send_ref):
    first = p_ref[0] == 0
    n, dt = n_ref[...], dt_ref[...]
    qk = mm_tn(n, dt[:, :256])
    vo = jnp.concatenate([mm_tn(n, dt[:, 256:]), mm_tn(db_ref[...], att_ref[...])], axis=1)
    send_ref[...] = jnp.where(first, vo, qk).astype(bf16)
    keep_ref[...] = jnp.where(first, qk, vo).astype(bf16)


def k_grad_sum(a_ref, b_ref, c_ref, d_ref, e_ref, f_ref, o_ref):
    at = 0
    for keep, got in ((a_ref, b_ref), (c_ref, d_ref), (e_ref, f_ref)):
        v = (keep[...].astype(f32) + got[...].astype(f32)).astype(bf16)
        o_ref[:, at : at + v.shape[1]] = v
        at += v.shape[1]


def exchange(x, axis):
    return lax.all_to_all(x, axis, 0, 0, tiled=True)


def swap(x):
    return lax.ppermute(x, "pipe", [(0, 1), (1, 0)])


def copies(x, n):
    return jnp.broadcast_to(x[None], (n, *x.shape))


def body(latents, cotangent, labels, steps, label_table, w_ada, w_qkv, w_out, w_up, w_down):
    p, t = lax.axis_index("pipe"), lax.axis_index("tp")
    first = p == 0
    who, part_no = p.astype(jnp.int32).reshape(1), t.astype(jnp.int32).reshape(1)
    width = latents.shape[2]

    def of_layer(own, other):
        return jnp.where(first, own, other), jnp.where(first, other, own)

    store = Store()
    slot = store.slot

    def run(kernel, outs, *args):
        return call(store, kernel, outs, *args)

    keep, send = run(
        k_halves, [((128, 768), bf16)] * 2,
        who, Near(w_qkv[0].transpose(1, 0, 2)), Near(w_out[0]), Near(w_up[0]), Near(w_down[0]),
    )
    half = width // 2
    freq = jnp.exp(-math.log(10000.0) * jnp.arange(half, dtype=f32) / half)
    angles = steps.astype(f32)[:, None] * freq[None, :]
    sinus = jnp.concatenate([jnp.cos(angles), jnp.sin(angles)], axis=1)
    ada = w_ada[0].transpose(1, 2, 0).reshape(96, width)
    packed, w0, w1, condition, cond_act = run(
        k_pack,
        [
            ((8, 160, 256), bf16), ((128, 512), bf16), ((128, 768), bf16),
            ((LAT, width), f32), ((LAT, width), bf16),
        ],
        who, part_no, labels, label_table, sinus, ada, keep, swap(send),
    )
    w0 = lax.all_gather(w0, "ctx", axis=0, tiled=True)
    packed = exchange(packed, "ctx")
    (spread,) = run(k_spread, [((8, 8, 32, 128), bf16)], packed)
    packed = packed.reshape(1280, 256)
    packed_other = swap(packed)
    sa = [[slot((1024, 256), bf16) for _ in range(2)] for _ in range(2)]
    sm = [[slot((1024, 512), bf16) for _ in range(2)] for _ in range(2)]
    wa0 = [Half(c, packed, packed_other, 160, 128, 0, 256, sa[0][c]) for c in range(2)]
    (mod_own,) = run(k_mods, [((32, 1024), bf16)], exchange(spread, "tp"))
    mods = run(k_two_layers, [((32, 1024), bf16)] * 2, who, mod_own, swap(mod_own))

    bc = ((8, 24, 1024), bf16)
    wide = ((192, 1024), bf16)
    kv_all = ((1536, 256), bf16)

    def rows24(n=24):
        return slot((n, 1024), f32)

    def rows192(n):
        return slot((192, n), bf16)

    def attn_forward(q, kv, w):
        kv_a = exchange(kv, "ctx").reshape(1536, 256)
        kv_b = swap(kv_a)
        att, sa, sb = rows192(128), slot((1536, 256), bf16), slot((1536, 256), bf16)
        (branch,) = run(k_attn, [att, wide], q, Save(kv_a, sa), Save(kv_b, sb), w[1])
        return (q, sa, sb, att), exchange(branch.reshape(8, 24, 1024), "tp")

    def attn_back(kept, normed, dbranch, w):
        q, kv_a, kv_b, att = kept
        db, dq, dt = rows192(1024), rows192(128), rows192(384)
        da, dp = run(k_attn_back, [dq, kv_all, kv_all], q, kv_a, kv_b, w[1], Save(dbranch, db))
        (both,) = run(k_pair_sum, [kv_all], da, swap(dp))
        arrived = exchange(both.reshape(8, 192, 256), "ctx")
        (dn,) = run(k_qkv_back, [dt, wide], dq, arrived, *w)
        arrived = exchange(dn.reshape(8, 24, 1024), "tp")
        keep = slot((1024, 256), bf16)
        (send,) = run(k_grad_attn, [keep, ((1024, 256), bf16)], who, normed, dt, db, att)
        return arrived, keep, swap(send)

    def grads_mlp(n, dpre, dm, hid):
        keep = slot((1024, 512), bf16)
        (send,) = run(k_grad_mlp, [keep, ((1024, 512), bf16)], who, n, dpre, dm, hid)
        return keep, swap(send)

    def to_rows(x):
        return exchange(x, "tp").reshape(192, 1024)

    x0, normed0, q0 = rows24(), rows192(1024), rows192(128)
    (kv,) = run(
        k_first, [x0, normed0, q0, ((8, 192, 256), bf16)],
        who, part_no, Near(latents), mods[0], *wa0,
    )
    wa0 = sa[0]
    cot, dm1 = rows24(), rows192(1024)
    run(k_gate_rows, [cot, dm1], who, part_no, Near(cotangent), mods[1])
    kept0, arrived = attn_forward(q0, kv, wa0)
    br0, mid0 = rows24(), rows24()
    (n2,) = run(k_mid, [br0, mid0, bc], arrived, x0, mods[0])
    n2 = to_rows(n2)
    w0_other = swap(w0)
    wm0 = [Half(c, w0, w0_other, 1024, 1024, 0, 512, sm[0][c]) for c in range(2)]
    n2_0, hid0 = rows192(1024), rows192(512)
    (out,) = run(k_mlp, [hid0, wide], Save(n2, n2_0), *wm0)
    wm0 = sm[0]
    arrived = exchange(out.reshape(8, 24, 1024), "tp")
    mlp0, x1 = rows24(), rows24()
    (n1,) = run(k_next, [mlp0, x1, bc], arrived, mid0, mods[0], mods[1])

    w1 = lax.all_gather(w1, "ctx", axis=0, tiled=True)
    n1, w1 = lax.optimization_barrier((n1, w1))
    n1 = to_rows(n1)
    w1_other = swap(w1)
    wa1 = [Half(c, w1, w1_other, 1024, 1024, 0, 256, sa[1][c]) for c in range(2)]
    wm1 = [Half(c, w1, w1_other, 1024, 1024, 256, 512, sm[1][c]) for c in range(2)]
    normed1, q1 = rows192(1024), rows192(128)
    (kv,) = run(k_qkv, [q1, ((8, 192, 256), bf16)], Save(n1, normed1), *wa1)
    wa1 = sa[1]
    kept1, arrived = attn_forward(q1, kv, wa1)
    br1, mid1 = rows24(), rows24()
    (n2,) = run(k_mid, [br1, mid1, bc], arrived, x1, mods[1])
    n2 = to_rows(n2)
    n2_1, hid1, dpre1 = rows192(1024), rows192(512), rows192(512)
    (both,) = run(
        k_mlp_both, [hid1, dpre1, ((8, 2, 24, 1024), bf16)], Save(n2, n2_1), *wm1, dm1
    )
    arrived = exchange(both, "tp")
    res1, dmid1, dmod1a = rows24(), rows24(), rows24(12)
    (db,) = run(k_last, [res1, dmid1, dmod1a, bc], arrived, mid1, br1, cot, mods[1])
    gm1 = grads_mlp(n2_1, dpre1, dm1, hid1)

    arrived, *ga1 = attn_back(kept1, normed1, to_rows(db), wa1)
    dx1, dmod1b = rows24(), rows24(6)
    (dm,) = run(k_back_one, [dx1, dmod1b, bc], arrived, x1, dmid1, mods[1], mods[0])
    dm = to_rows(dm)

    dm0, dpre0 = rows192(1024), rows192(512)
    (dn,) = run(k_mlp_back, [dpre0, wide], n2_0, *wm0, Save(dm, dm0))
    arrived = exchange(dn.reshape(8, 24, 1024), "tp")
    gm0 = grads_mlp(n2_0, dpre0, dm0, hid0)
    dmid0, dmod0a = rows24(), rows24(12)
    (db,) = run(k_back_two, [dmid0, dmod0a, bc], arrived, mid0, br0, dx1, mlp0, mods[0])
    (mixed,) = run(k_grad_sum, [((1024, 1280), bf16)], *gm0, *gm1, *ga1)
    mixed = lax.psum_scatter(mixed, "ctx", tiled=True)
    gm0, gm1, ga1 = mixed[:, :512], mixed[:, 512:1024], mixed[:, 1024:]

    arrived, *ga0 = attn_back(kept0, normed0, to_rows(db), wa0)
    keep, send = run(
        k_back_first, [((48, 1024), f32)] * 2,
        who, arrived, x0, dmid0, mods[0], dmod0a, dmod1a, dmod1b, res1,
    )

    (tail,) = run(k_tail_tp, [((8, 72, 1024), bf16)], who, keep, swap(send))
    tail = exchange(tail, "tp")
    (tail_ctx,) = run(k_tail_ctx, [((8, 160, 256), bf16)], tail, *ga0)
    tail_ctx = exchange(tail_ctx, "ctx")
    (ends,) = run(k_ends, [((LAT, 128, 1024), f32)], tail)
    ga0, grad_ada, cond_part = run(
        k_cond, [((128, 256), bf16), ((96, 1024), f32), ((LAT, 1024), f32)],
        part_no, tail_ctx, cond_act, ada,
    )
    cond_part = (cond_part + swap(cond_part)).reshape(24, 128)
    grad_act = exchange(copies(cond_part, 64), ("ctx", "tp"))
    mine = jnp.concatenate([jnp.where(first, gm0, gm1), jnp.where(first, ga0, ga1)], axis=1)
    send = jnp.concatenate([jnp.where(first, gm1, gm0), jnp.where(first, ga1, ga0)], axis=1)
    half0, half1 = of_layer(mine, swap(send))
    grad_up = half0[:, :512].astype(f32)
    grad_down = half1[:, :512].astype(f32).T
    grad_qkv = jnp.concatenate([half0[:, 512:], half1[:, 512:640]], axis=1).astype(f32)
    grad_out = half1[:, 640:].astype(f32).T

    grad_act, grad_up, grad_down, grad_qkv, grad_out = lax.optimization_barrier(
        (grad_act, grad_up, grad_down, grad_qkv, grad_out)
    )
    grad_act = grad_act.sum(axis=0).reshape(LAT, width)
    sig = jax.nn.sigmoid(condition)
    grad_cond = grad_act * (sig * (1.0 + condition * (1.0 - sig)))
    classes = jnp.arange(label_table.shape[0], dtype=jnp.int32)[:, None]
    grad_table = sum(
        jnp.where(classes == labels[l], grad_cond[l : l + 1], 0.0) for l in range(LAT)
    )

    return (
        ends[None],
        grad_table,
        grad_ada.reshape(6, 16, width).transpose(2, 0, 1)[None],
        grad_qkv.reshape(1, 128, 3, 128),
        grad_out[None],
        grad_up[None],
        grad_down[None],
    )


def solution(mesh):
    return jax.shard_map(
        body,
        mesh=mesh,
        in_specs=(
            P(None, "ctx", None),
            P(None, "ctx", None),
            P(),
            P(),
            P(),
            P("pipe", None, None, ("ctx", "tp")),
            P("pipe", "ctx", None, "tp"),
            P("pipe", "tp", "ctx"),
            P("pipe", "ctx", "tp"),
            P("pipe", "tp", "ctx"),
        ),
        out_specs=(
            P("pipe", None, "ctx", None),
            P(),
            P("pipe", None, None, ("ctx", "tp")),
            P("pipe", "ctx", None, "tp"),
            P("pipe", "tp", "ctx"),
            P("pipe", "ctx", "tp"),
            P("pipe", "tp", "ctx"),
        ),
        check_vma=False,
    )
```

```python
import math

import jax
import jax.numpy as jnp
from jax import lax
from jax.experimental import pallas as pl
from jax.experimental.pallas import tpu as pltpu
from jax.sharding import PartitionSpec as P


LAT = 3
HEAD = 64
EPS = 1e-06
GELU_C = math.sqrt(2.0 / math.pi)
GELU_A = 0.044715
STORE_ROWS = 34048

f32 = jnp.float32
bf16 = jnp.bfloat16


def sds(shape, dtype):
    return jax.ShapeDtypeStruct(shape, dtype)


def up16(n):
    return -(-n // 16) * 16


class Slot:
    def __init__(self, row, shape, dtype):
        self.row, self.shape, self.dtype = row, shape, dtype
        self.rows = up16(shape[0]) * (2 if dtype == f32 else 1)

    def of(self, ref):
        return ref.at[pl.ds(self.row, self.rows), pl.ds(0, self.shape[1])]


class Store:
    def __init__(self):
        self.array, self.next = None, 0

    def slot(self, shape, dtype):
        s = Slot(self.next, shape, dtype)
        self.next += s.rows
        assert self.next <= STORE_ROWS
        return s


class Save:
    def __init__(self, array, slot):
        self.array, self.slot = array, slot


class Near:
    def __init__(self, array):
        self.array = array


class Half:
    def __init__(self, core, own, other, block, rows, at, width, slot):
        self.core, self.own, self.other = core, own, other
        self.block, self.rows, self.at, self.width, self.slot = block, rows, at, width, slot


class Held:
    def __init__(self, ref, wait, shape, dtype):
        self.ref, self.wait, self.shape, self.dtype = ref, wait, shape, dtype

    def ready(self):
        if self.wait is not None:
            self.wait()
            self.wait = None

    def __getitem__(self, at):
        self.ready()
        if self.dtype != f32 or self.ref.dtype == f32:
            return self.ref[at]
        n = self.shape[0]
        low = up16(n)
        return self.ref[:n].astype(f32) + self.ref[low : low + n].astype(f32)


class Kept:
    def __init__(self, ref, copy, shape, dtype):
        self.ref, self.copy, self.shape, self.dtype, self.gone = ref, copy, shape, dtype, False

    def send(self):
        if not self.gone:
            self.copy.start()
            self.gone = True

    def __setitem__(self, at, v):
        if self.dtype == f32:
            n = self.shape[0]
            low = up16(n)
            high = v.astype(bf16)
            self.ref[:n] = high
            self.ref[low : low + n] = (v - high.astype(f32)).astype(bf16)
            self.send()
        else:
            self.ref[at] = v
            if at is Ellipsis:
                self.send()


def ready(*refs):
    for r in refs:
        if isinstance(r, Held):
            r.ready()


def call(store, kernel, outs, *args, alone=False):
    vmem = pl.BlockSpec(memory_space=pltpu.VMEM)
    smem = pl.BlockSpec(memory_space=pltpu.SMEM)
    far = pl.BlockSpec(memory_space=pltpu.HBM)
    uses = any(isinstance(a, (Slot, Save, Half)) for a in args) or any(
        isinstance(o, Slot) for o in outs
    )
    flat, in_specs, plan, scratch = [], [], [], []

    def hold(shape, dtype):
        scratch.append(pltpu.VMEM(shape, dtype))
        return len(scratch) - 1

    for a in args:
        if isinstance(a, Slot):
            plan.append(("slot", a, hold((a.rows, a.shape[1]), bf16)))
        elif isinstance(a, Near):
            plan.append(("near", len(flat), hold(a.array.shape, a.array.dtype)))
            flat.append(a.array)
            in_specs.append(far)
        elif isinstance(a, Half):
            plan.append(("half", len(flat), hold(a.slot.shape, bf16), a))
            flat += [a.own, a.other]
            in_specs += [far, far]
        else:
            v = a.array if isinstance(a, Save) else a
            plan.append(("here", len(flat), a))
            flat.append(v)
            in_specs.append(smem if v.dtype == jnp.int32 else vmem)
    out_shape, out_specs, out_plan = [], [], []
    for o in outs:
        if isinstance(o, Slot):
            out_plan.append((o, hold((o.rows, o.shape[1]), bf16)))
        elif alone:
            out_plan.append((len(out_shape), hold(*o)))
            out_shape.append(sds(*o))
            out_specs.append(far)
        else:
            out_plan.append((None, len(out_shape)))
            out_shape.append(sds(*o))
            out_specs.append(vmem)
    n_args, n_out, n_hold = len(flat), len(out_shape), len(scratch)
    n_saves = sum(isinstance(a, (Save, Half)) for a in args)
    alias = {}
    if uses:
        if store.array is not None:
            flat.append(store.array)
            in_specs.append(far)
            alias = {len(flat) - 1: n_out}
        out_shape.append(sds((STORE_ROWS, 1024), bf16))
        out_specs.append(far)
    n_in = len(flat)
    n_sems = n_hold + n_saves

    def wrapped(*refs):
        ins, results = refs[:n_in], refs[n_in : n_in + len(out_shape)]
        holds = refs[n_in + len(out_shape) :]
        sems = holds[n_hold] if n_sems else None
        big = results[n_out] if uses else None
        given, leaving, late = [], [], n_hold
        for item in plan:
            if item[0] == "here":
                given.append(ins[item[1]])
                if isinstance(item[2], Save):
                    copy = pltpu.make_async_copy(ins[item[1]], item[2].slot.of(big), sems.at[late])
                    copy.start()
                    leaving.append(copy)
                    late += 1
                continue
            to, sem = holds[item[2]], sems.at[item[2]]
            if item[0] == "half":
                h = item[3]
                mine = lax.axis_index("pipe") == h.core
                for k in range(2):

                    @pl.when(mine if k == 0 else jnp.logical_not(mine))
                    def _(src=ins[item[1] + k]):
                        for c in range(h.slot.shape[0] // h.rows):
                            pltpu.make_async_copy(
                                src.at[pl.ds(c * h.block, h.rows), pl.ds(h.at, h.width)],
                                to.at[pl.ds(c * h.rows, h.rows)],
                                sem,
                            ).start()

                whole = pltpu.make_async_copy(to, to, sem)
                out = pltpu.make_async_copy(to, h.slot.of(big), sems.at[late])
                late += 1
                leaving.append(out)

                def arrive(whole=whole, out=out):
                    whole.wait()
                    out.start()

                given.append(Held(to, arrive, h.slot.shape, bf16))
                continue
            if item[0] == "slot":
                copy = pltpu.make_async_copy(item[1].of(big), to, sem)
                shape, dtype = item[1].shape, item[1].dtype
            else:
                copy = pltpu.make_async_copy(ins[item[1]], to, sem)
                shape, dtype = to.shape, to.dtype
            copy.start()
            given.append(Held(to, copy.wait, shape, dtype))
        for slot, at in out_plan:
            if slot is None:
                given.append(results[at])
            else:
                if isinstance(slot, Slot):
                    copy = pltpu.make_async_copy(holds[at], slot.of(big), sems.at[at])
                    kept = Kept(holds[at], copy, slot.shape, slot.dtype)
                else:
                    copy = pltpu.make_async_copy(holds[at], results[slot], sems.at[at])
                    kept = Kept(holds[at], copy, None, None)
                leaving.append(copy)
                given.append(kept)
        kernel(*given)
        ready(*given)
        for g in given:
            if isinstance(g, Kept):
                g.send()
        for copy in leaving:
            copy.wait()

    got = pl.pallas_call(
        wrapped,
        out_shape=tuple(out_shape),
        in_specs=in_specs,
        out_specs=tuple(out_specs),
        scratch_shapes=scratch + ([pltpu.SemaphoreType.DMA((n_sems,))] if n_sems else []),
        input_output_aliases=alias,
        compiler_params=pltpu.CompilerParams(vmem_limit_bytes=(60 if alone else 24) * 1024 * 1024),
    )(*flat)
    if uses:
        store.array = got[n_out]
    return got[:n_out]


def mm(a, b):
    return lax.dot_general(a, b, (((1,), (0,)), ((), ())), preferred_element_type=f32)


def mm_nt(a, b):
    return lax.dot_general(a, b, (((1,), (1,)), ((), ())), preferred_element_type=f32)


def mm_tn(a, b):
    return lax.dot_general(a, b, (((0,), (0,)), ((), ())), preferred_element_type=f32)


def part(mod, k):
    return jnp.concatenate(
        [jnp.broadcast_to(mod[3 * k + l : 3 * k + l + 1, :], (8, mod.shape[1])) for l in range(LAT)],
        axis=0,
    )


def centred(x):
    c = x - jnp.mean(x, axis=-1, keepdims=True)
    r = lax.rsqrt(jnp.mean(c * c, axis=-1, keepdims=True) + EPS)
    return c * r, r


def norm_back(x, dy, scale):
    xh, r = centred(x)
    g = dy * (1.0 + scale)
    dx = r * (
        g - jnp.mean(g, axis=-1, keepdims=True) - xh * jnp.mean(g * xh, axis=-1, keepdims=True)
    )
    return dx, dy, dy * xh


def row_sums(*vs):
    return jnp.concatenate(
        [jnp.sum(v[8 * l : 8 * l + 8], axis=0, keepdims=True) for v in vs for l in range(LAT)], axis=0
    )


def summed(ref, *at):
    total = ref[(0, *at)].astype(f32)
    for j in range(1, 8):
        total = total + ref[(j, *at)].astype(f32)
    return total


def to_all(ref, v):
    for j in range(8):
        ref[j] = v


def by_latent(v):
    v = v.reshape(8, LAT, 8, v.shape[-1])
    return [v[:, l].reshape(64, v.shape[-1]) for l in range(LAT)]


def rows_of(v):
    return v.reshape(-1, v.shape[-1])


def by_part(vs):
    w = vs[0].shape[-1]
    return jnp.stack([v.reshape(8, 8, w) for v in vs], axis=1).reshape(192, w)


def gelu_parts(x):
    t = jnp.tanh(GELU_C * (x + GELU_A * (x * x * x)))
    return t


def k_halves(p_ref, wq_ref, wo_ref, up_ref, down_ref, keep_ref, send_ref):
    ready(wq_ref, wo_ref, up_ref, down_ref)

    a = jnp.concatenate([wq_ref[0], wq_ref[1], up_ref[...]], axis=1).astype(f32)
    wo, down = wo_ref[...].astype(f32).T, down_ref[...].astype(f32).T
    b = jnp.concatenate([wq_ref[2].astype(f32), wo, down], axis=1)
    first = p_ref[0] == 0
    send_ref[...] = jnp.where(first, b, a).astype(bf16)
    keep_ref[...] = jnp.where(first, a, b).astype(bf16)


def k_pack(
    p_ref, t_ref, lab_ref, table_ref, sinus_ref, ada_ref, keep_ref, got_ref,
    o_ref, w0_ref, w1_ref, cond_ref, act_ref,
):
    first = p_ref[0] == 0
    keep, got = keep_ref[...].astype(f32), got_ref[...].astype(f32)
    w0 = jnp.where(first, keep, got).astype(bf16)
    w0_ref[...] = w0[:, 256:]
    w1_ref[...] = jnp.where(first, got, keep).astype(bf16)
    row = lax.broadcasted_iota(jnp.int32, (8, table_ref.shape[0]), 0)
    col = lax.broadcasted_iota(jnp.int32, (8, table_ref.shape[0]), 1)
    label = jnp.where(row == 0, lab_ref[0], jnp.where(row == 1, lab_ref[1], lab_ref[2]))
    cond = mm(jnp.where(col == label, 1.0, 0.0).astype(bf16), table_ref[...])[:LAT] + sinus_ref[...]
    cond_ref[...] = cond
    act = (cond / (1.0 + jnp.exp(-cond))).astype(bf16)
    act_ref[...] = act
    row = lax.broadcasted_iota(jnp.int32, (96, 768), 0)
    lane = lax.broadcasted_iota(jnp.int32, (96, 768), 1)
    to = 128 * (row // 16) + row % 16 + 16 * t_ref[0]
    place = jnp.where(lane == to, 1.0, 0.0).astype(bf16)
    mod = mm(mm_nt(act, ada_ref[...]).astype(bf16), place)
    mod = jnp.concatenate([mod[:, 128 * k : 128 * k + 128] for k in range(6)], axis=0)
    mod = jnp.concatenate([mod, jnp.zeros((14, 128), f32)], axis=0)
    mod = jnp.concatenate([mod, jnp.zeros((32, 128), f32)], axis=1).astype(bf16)
    for j in range(8):
        o_ref[j, :128] = w0[:, :256]
        o_ref[j, 128:] = mod


def k_spread(r_ref, o_ref):
    for c in range(8):
        v = r_ref[c, 128:, :128][:24]
        for j in range(8):
            o_ref[j, c] = v


def k_mods(r_ref, o_ref):
    for c in range(8):
        o_ref[:, 128 * c : 128 * c + 128] = summed(r_ref, c).astype(bf16)


def k_two_layers(p_ref, own_ref, other_ref, a_ref, b_ref):
    own, other, first = own_ref[...].astype(f32), other_ref[...].astype(f32), p_ref[0] == 0
    a_ref[...] = jnp.where(first, own, other).astype(bf16)
    b_ref[...] = jnp.where(first, other, own).astype(bf16)


def put_qkv(y, q_ref, kv_ref):
    y = jnp.concatenate(by_latent(y), axis=0).astype(bf16)
    q_ref[...] = y[:, :128]
    to_all(kv_ref, y[:, 128:])


def triple(n, wa_ref, wb_ref):
    a = mm(n, rows_of(wa_ref[...]))
    return jnp.concatenate([a, mm(n, rows_of(wb_ref[...])[:, :128])], axis=1)


def k_rows(p_ref, t_ref, x_ref, c_ref, x_all_ref, x_own_ref, c_all_ref, c_own_ref):
    start = pl.multiple_of(64 * p_ref[0], 64)
    few = pl.multiple_of(64 * p_ref[0] + 8 * t_ref[0], 8)
    ready(x_ref, c_ref)
    for ref, all_ref, own_ref in ((x_ref.ref, x_all_ref, x_own_ref), (c_ref.ref, c_all_ref, c_own_ref)):
        blocks = [ref[l, pl.ds(start, 64), :] for l in range(LAT)]
        all_ref[...] = jnp.concatenate(
            [b[8 * j : 8 * j + 8] for j in range(8) for b in blocks], axis=0
        )
        own_ref[...] = jnp.concatenate([ref[l, pl.ds(few, 8), :] for l in range(LAT)], axis=0)


def k_first(x_ref, mod_ref, wa_ref, wb_ref, n_ref, q_ref, kv_ref):
    mod = mod_ref[...].astype(f32)
    shift, scale = part(mod, 0), 1.0 + part(mod, 1)
    x = x_ref[...]
    rows = [centred(x[24 * j : 24 * j + 24])[0] * scale + shift for j in range(8)]
    n = jnp.concatenate(rows, axis=0).astype(bf16)
    n_ref[...] = n
    put_qkv(triple(n, wa_ref, wb_ref), q_ref, kv_ref)


def k_qkv(n_ref, wa_ref, wb_ref, q_ref, kv_ref):
    put_qkv(triple(n_ref[...], wa_ref, wb_ref), q_ref, kv_ref)


def head_rows(v):
    lane = lax.broadcasted_iota(jnp.int32, v.shape, 1)
    zero = jnp.zeros_like(v)
    return jnp.concatenate(
        [jnp.where(lane < HEAD, v, zero), jnp.where(lane < HEAD, zero, v)], axis=0
    )


def head_lanes(v):
    lane = lax.broadcasted_iota(jnp.int32, (64, 128), 1)
    return jnp.where(lane < HEAD, v[:64], v[64:])


def keys_values(a_ref, b_ref, l):
    at = [64 * (LAT * c + l) for c in range(8)]
    kv = jnp.concatenate([r[i : i + 64] for r in (a_ref, b_ref) for i in at], axis=0)
    return kv[:, :128], kv[:, 128:]


def soft(qs, k):
    s = mm_nt(k, qs) * 0.125
    e = jnp.exp(s - jnp.max(s, axis=0, keepdims=True))
    return e * (1.0 / jnp.sum(e, axis=0, keepdims=True))


def k_attn(q_ref, a_ref, b_ref, w_ref, att_ref, o_ref):
    outs = []
    for l in range(LAT):
        k, v = keys_values(a_ref, b_ref, l)
        probs = soft(head_rows(q_ref[64 * l : 64 * l + 64].astype(f32)).astype(bf16), k)
        outs.append(head_lanes(mm_tn(probs.astype(bf16), v)))
    att = by_part(outs).astype(bf16)
    att_ref[...] = att
    o_ref[...] = mm_nt(att, rows_of(w_ref[...])[:, 128:]).astype(bf16)


def k_attn_back(q_ref, a_ref, b_ref, w_ref, db_ref, dq_ref, da_ref, dp_ref):
    datt = by_latent(mm(db_ref[...], rows_of(w_ref[...])[:, 128:]))
    for l in range(LAT):
        k, v = keys_values(a_ref, b_ref, l)
        qs = head_rows(q_ref[64 * l : 64 * l + 64].astype(f32)).astype(bf16)
        do = head_rows(datt[l]).astype(bf16)
        probs = soft(qs, k)
        dprobs = mm_nt(v, do)
        dv = mm(probs.astype(bf16), do)
        ds = probs * (dprobs - jnp.sum(probs * dprobs, axis=0, keepdims=True))
        ds = ds.astype(bf16)
        dk = mm(ds, qs) * 0.125
        dq_ref[64 * l : 64 * l + 64] = (head_lanes(mm_tn(ds, k)) * 0.125).astype(bf16)
        dkv = jnp.concatenate([dk, dv], axis=1).astype(bf16)
        for c in range(8):
            at = 64 * (LAT * c + l)
            da_ref[at : at + 64] = dkv[64 * c : 64 * c + 64]
            dp_ref[at : at + 64] = dkv[512 + 64 * c : 512 + 64 * c + 64]


def k_pair_sum(a_ref, b_ref, o_ref):
    o_ref[...] = (a_ref[...].astype(f32) + b_ref[...].astype(f32)).astype(bf16)


def k_qkv_back(dq_ref, r_ref, wa_ref, wb_ref, dt_ref, o_ref):
    dt = jnp.concatenate([dq_ref[...].astype(f32), summed(r_ref)], axis=1)
    dt = by_part([dt[64 * l : 64 * l + 64] for l in range(LAT)]).astype(bf16)
    dt_ref[...] = dt
    back = mm_nt(dt[:, :256], rows_of(wa_ref[...])) + mm_nt(dt[:, 256:], rows_of(wb_ref[...])[:, :128])
    o_ref[...] = back.astype(bf16)


def k_mid(r_ref, x_ref, mod_ref, br_ref, mid_ref, o_ref):
    mod = mod_ref[...].astype(f32)
    branch = summed(r_ref)
    mid = x_ref[...] + part(mod, 2) * branch
    br_ref[...] = branch
    mid_ref[...] = mid
    xh, _ = centred(mid)
    to_all(o_ref, (xh * (1.0 + part(mod, 4)) + part(mod, 3)).astype(bf16))


def k_mlp(n_ref, up_ref, down_ref, hid_ref, o_ref):
    pre = mm(n_ref[...], rows_of(up_ref[...]))
    hid = (0.5 * pre * (1.0 + gelu_parts(pre))).astype(bf16)
    hid_ref[...] = hid
    o_ref[...] = mm_nt(hid, rows_of(down_ref[...])).astype(bf16)


def gelu_slope(pre, t):
    inner = GELU_C * (1.0 + 3.0 * GELU_A * pre * pre)
    return 0.5 * (1.0 + t) + 0.5 * pre * (1.0 - t * t) * inner


def k_mlp_both(n_ref, up_ref, down_ref, dm_ref, hid_ref, dpre_ref, o_ref):
    pre = mm(n_ref[...], rows_of(up_ref[...]))
    t = gelu_parts(pre)
    hid = (0.5 * pre * (1.0 + t)).astype(bf16)
    hid_ref[...] = hid
    out = mm_nt(hid, rows_of(down_ref[...])).astype(bf16)
    dhid = mm(dm_ref[...], rows_of(down_ref[...]))
    dpre = (dhid * gelu_slope(pre, t)).astype(bf16)
    dpre_ref[...] = dpre
    back = mm_nt(dpre, rows_of(up_ref[...])).astype(bf16)
    for j in range(8):
        o_ref[j, 0] = out[24 * j : 24 * j + 24]
        o_ref[j, 1] = back[24 * j : 24 * j + 24]


def k_mlp_back(n_ref, up_ref, down_ref, dm_ref, dpre_ref, o_ref):
    pre = mm(n_ref[...], rows_of(up_ref[...]))
    dhid = mm(dm_ref[...], rows_of(down_ref[...]))
    dpre = (dhid * gelu_slope(pre, gelu_parts(pre))).astype(bf16)
    dpre_ref[...] = dpre
    o_ref[...] = mm_nt(dpre, rows_of(up_ref[...])).astype(bf16)


def k_gate_rows(c_ref, mod_ref, o_ref):
    gate = part(mod_ref[...].astype(f32), 5)
    c = c_ref[...]
    rows = [gate * c[24 * j : 24 * j + 24] for j in range(8)]
    o_ref[...] = jnp.concatenate(rows, axis=0).astype(bf16)


def k_next(r_ref, mid_ref, mod_ref, mod_next_ref, mlp_ref, x_ref, o_ref):
    mod, mod_next = mod_ref[...].astype(f32), mod_next_ref[...].astype(f32)
    mlp = summed(r_ref)
    mlp_ref[...] = mlp
    x = mid_ref[...] + part(mod, 5) * mlp
    x_ref[...] = x
    xh, _ = centred(x)
    to_all(o_ref, (xh * (1.0 + part(mod_next, 1)) + part(mod_next, 0)).astype(bf16))


def back_two(mod, mid, branch, dy, dn, mlp, dmid_ref, dmod_ref, o_ref):
    dx, ds, dc = norm_back(mid, dn, part(mod, 4))
    dmid = dy + dx
    dmid_ref[...] = dmid
    to_all(o_ref, (part(mod, 2) * dmid).astype(bf16))
    dmod_ref[...] = row_sums(dmid * branch, ds, dc, dy * mlp)


def k_last(r_ref, mid_ref, br_ref, dy_ref, mod_ref, res_ref, dmid_ref, dmod_ref, o_ref):
    mod = mod_ref[...].astype(f32)
    mlp, dn = summed(r_ref, 0), summed(r_ref, 1)
    mid = mid_ref[...]
    res_ref[...] = mid + part(mod, 5) * mlp
    back_two(mod, mid, br_ref[...], dy_ref[...], dn, mlp, dmid_ref, dmod_ref, o_ref)


def k_back_two(r_ref, mid_ref, br_ref, dy_ref, mlp_ref, mod_ref, dmid_ref, dmod_ref, o_ref):
    mod = mod_ref[...].astype(f32)
    back_two(
        mod, mid_ref[...], br_ref[...], dy_ref[...], summed(r_ref), mlp_ref[...],
        dmid_ref, dmod_ref, o_ref,
    )


def k_back_one(r_ref, x_ref, dmid_ref, mod_ref, mod_before_ref, dx_ref, dmod_ref, o_ref):
    dx, ds, dc = norm_back(x_ref[...], summed(r_ref), part(mod_ref[...].astype(f32), 1))
    dx = dmid_ref[...] + dx
    dx_ref[...] = dx
    dmod_ref[...] = row_sums(ds, dc)
    to_all(o_ref, (part(mod_before_ref[...].astype(f32), 5) * dx).astype(bf16))


def k_back_first(
    p_ref, r_ref, x_ref, dmid_ref, mod_ref, d0_ref, d1a_ref, d1b_ref, res_ref, keep_ref, send_ref
):
    first = p_ref[0] == 0
    dx, ds, dc = norm_back(x_ref[...], summed(r_ref), part(mod_ref[...].astype(f32), 1))
    dx = dmid_ref[...] + dx
    res = res_ref[...]
    keep_ref[:24] = jnp.where(first, dx, res)
    send_ref[:24] = jnp.where(first, res, dx)
    none = jnp.zeros((6, dx.shape[1]), f32)
    d0 = jnp.concatenate([row_sums(ds, dc), d0_ref[...], none], axis=0)
    d1 = jnp.concatenate([d1b_ref[...], d1a_ref[...], none], axis=0)
    keep_ref[24:] = jnp.where(first, d0, d1)
    send_ref[24:] = jnp.where(first, d1, d0)


def k_tail_tp(p_ref, keep_ref, got_ref, o_ref):
    first = p_ref[0] == 0
    keep, got = keep_ref[...], got_ref[...]
    v = jnp.concatenate(
        [
            jnp.where(first, keep[:24], got[:24]),
            jnp.where(first, got[:24], keep[:24]),
            keep[24:] + got[24:],
        ],
        axis=0,
    ).astype(bf16)
    to_all(o_ref, v)


def k_tail_ctx(r_ref, a_ref, b_ref, o_ref):
    total = r_ref[0].astype(f32)[48:]
    for j in range(1, 8):
        total = total + r_ref[j].astype(f32)[48:]
    total = jnp.concatenate([total, jnp.zeros((8, total.shape[1]), f32)], axis=0).astype(bf16)
    none = jnp.zeros((32, 128), bf16)
    for c in range(8):
        at = slice(128 * c, 128 * c + 128)
        o_ref[c, :128, :] = (a_ref[at].astype(f32) + b_ref[at].astype(f32)).astype(bf16)
        o_ref[c, 128:160, :128] = total[:, at]
        o_ref[c, 128:160, 128:] = none


def k_ends(r_ref, o_ref):
    for j in range(8):
        v = r_ref[j].astype(f32)
        for half in range(2):
            for l in range(LAT):
                at = 64 * half + 8 * j
                o_ref[l, at : at + 8, :] = v[24 * half + 8 * l : 24 * half + 8 * l + 8]


def k_cond(t_ref, r_ref, act_ref, ada_ref, g_ref, ada_grad_ref, o_ref):
    total = summed(r_ref)
    d = total[128:, :128].astype(bf16)
    lane = lax.broadcasted_iota(jnp.int32, (128, 16), 0)
    col = lax.broadcasted_iota(jnp.int32, (128, 16), 1)
    pick = jnp.where(lane == col + 16 * t_ref[0], 1.0, 0.0).astype(bf16)
    d = mm(d, pick)
    act = act_ref[...]
    c = jnp.zeros(act.shape, f32)
    for k in range(6):
        dk = d[3 * k : 3 * k + 3].astype(bf16)
        ada_grad_ref[16 * k : 16 * k + 16, :] = mm_tn(dk, act)
        c = c + mm(dk, ada_ref[16 * k : 16 * k + 16, :])
    v = [c[l : l + 1, 128 * k : 128 * k + 128] for l in range(LAT) for k in range(8)]
    v = jnp.concatenate(v, axis=0).astype(bf16)
    for j in range(64):
        o_ref[j] = v
    g_ref[...] = total[:128].astype(bf16)


def k_final_send(p_ref, m0_ref, m1_ref, o_ref):
    m0, m1 = m0_ref[...].astype(f32), m1_ref[...].astype(f32)
    o_ref[:, :512] = jnp.where(p_ref[0] == 0, m1[:, :512], m0).astype(bf16)
    o_ref[:, 512:] = m1[:, 512:].astype(bf16)


def k_final(p_ref, m0_ref, m1_ref, a_ref, g_ref, b_ref, up_ref, down_ref, qkv_ref, out_ref):
    first = p_ref[0] == 0
    m0, m1, a = (r[...].astype(f32) for r in (m0_ref, m1_ref, a_ref))
    g, b = g_ref[...].astype(f32), b_ref[...].astype(f32)
    up_ref[...] = jnp.where(first, m0, a[:, :512])
    down_ref[...] = jnp.where(first, a[:, :512], m1[:, :512]).T
    qk = jnp.where(first, g, a[:, 512:])
    vo = jnp.where(first, b, m1[:, 512:])
    qkv_ref[0], qkv_ref[1], qkv_ref[2] = qk[:, :128], qk[:, 128:], vo[:, :128]
    out_ref[...] = vo[:, 128:].T


def k_grad_mlp(p_ref, n_ref, dpre_ref, dm_ref, hid_ref, keep_ref, send_ref):
    first = p_ref[0] == 0
    n, dm = n_ref[...], dm_ref[...]
    dpre, hid = dpre_ref[...], hid_ref[...]

    def pick(a, b):
        return jnp.where(first, a.astype(f32), b.astype(f32)).astype(bf16)

    send_ref[...] = mm_tn(pick(dm, n), pick(hid, dpre)).astype(bf16)
    keep_ref[...] = mm_tn(pick(n, dm), pick(dpre, hid)).astype(bf16)


def k_grad_attn(p_ref, n_ref, dt_ref, db_ref, att_ref, keep_ref, send_ref):
    first = p_ref[0] == 0
    n, dt = n_ref[...], dt_ref[...]
    qk = mm_tn(n, dt[:, :256])
    vo = jnp.concatenate([mm_tn(n, dt[:, 256:]), mm_tn(db_ref[...], att_ref[...])], axis=1)
    send_ref[...] = jnp.where(first, vo, qk).astype(bf16)
    keep_ref[...] = jnp.where(first, qk, vo).astype(bf16)


def k_grad_sum(*refs):
    o_ref, at = refs[-1], 0
    for keep, got in zip(refs[0:-1:2], refs[1:-1:2]):
        v = (keep[...].astype(f32) + got[...].astype(f32)).astype(bf16)
        o_ref[:, at : at + v.shape[1]] = v
        at += v.shape[1]


def exchange(x, axis):
    return lax.all_to_all(x, axis, 0, 0, tiled=True)


def swap(x):
    return lax.ppermute(x, "pipe", [(0, 1), (1, 0)])


def body(latents, cotangent, labels, steps, label_table, w_ada, w_qkv, w_out, w_up, w_down):
    p, t = lax.axis_index("pipe"), lax.axis_index("tp")
    who, part_no = p.astype(jnp.int32).reshape(1), t.astype(jnp.int32).reshape(1)
    width = latents.shape[2]

    store = Store()
    slot = store.slot

    def run(kernel, outs, *args, alone=False):
        return call(store, kernel, outs, *args, alone=alone)

    keep, send = run(
        k_halves, [((128, 768), bf16)] * 2,
        who, Near(w_qkv[0].transpose(1, 0, 2)), Near(w_out[0]), Near(w_up[0]), Near(w_down[0]),
        alone=True,
    )
    half = width // 2
    freq = jnp.exp(-math.log(10000.0) * jnp.arange(half, dtype=f32) / half)
    angles = steps.astype(f32)[:, None] * freq[None, :]
    sinus = jnp.concatenate([jnp.cos(angles), jnp.sin(angles)], axis=1)
    ada = w_ada[0].transpose(1, 2, 0).reshape(96, width)
    packed, w0, w1, condition, cond_act = run(
        k_pack,
        [
            ((8, 160, 256), bf16), ((128, 512), bf16), ((128, 768), bf16),
            ((LAT, width), f32), ((LAT, width), bf16),
        ],
        who, part_no, labels, Near(label_table), Near(sinus), Near(ada), Near(keep), Near(swap(send)),
        alone=True,
    )
    w0 = lax.all_gather(w0, "ctx", axis=0, tiled=True)
    packed = exchange(packed, "ctx")
    packed, latents, cotangent = lax.optimization_barrier((packed, latents, cotangent))
    (spread,) = run(k_spread, [((8, 8, 24, 128), bf16)], packed)
    packed = packed.reshape(1280, 256)
    packed_other = swap(packed)
    sa = [[slot((1024, 256), bf16) for _ in range(2)] for _ in range(2)]
    sm = [[slot((1024, 512), bf16) for _ in range(2)] for _ in range(2)]
    wa0 = [Half(c, packed, packed_other, 160, 128, 0, 256, sa[0][c]) for c in range(2)]
    x_all, x0 = slot((192, 1024), f32), slot((24, 1024), f32)
    cot_all, cot = slot((192, 1024), f32), slot((24, 1024), f32)
    run(k_rows, [x_all, x0, cot_all, cot], who, part_no, Near(latents), Near(cotangent), alone=True)
    spread, store.array = lax.optimization_barrier((exchange(spread, "tp"), store.array))
    (mod_own,) = run(k_mods, [((24, 1024), bf16)], spread)
    mods = run(k_two_layers, [((24, 1024), bf16)] * 2, who, mod_own, swap(mod_own))

    bc = ((8, 24, 1024), bf16)
    wide = ((192, 1024), bf16)
    kv_all = ((1536, 256), bf16)

    def rows24(n=24):
        return slot((n, 1024), f32)

    def rows192(n):
        return slot((192, n), bf16)

    def attn_forward(q, kv, w):
        kv_a = exchange(kv, "ctx").reshape(1536, 256)
        kv_b = swap(kv_a)
        att, sa, sb = rows192(128), slot((1536, 256), bf16), slot((1536, 256), bf16)
        (branch,) = run(k_attn, [att, wide], q, Save(kv_a, sa), Save(kv_b, sb), w[1])
        return (q, sa, sb, att), exchange(branch.reshape(8, 24, 1024), "tp")

    def attn_back(kept, normed, dbranch, w):
        q, kv_a, kv_b, att = kept
        db, dq, dt = rows192(1024), rows192(128), rows192(384)
        da, dp = run(k_attn_back, [dq, kv_all, kv_all], q, kv_a, kv_b, w[1], Save(dbranch, db))
        (both,) = run(k_pair_sum, [kv_all], da, swap(dp))
        arrived = exchange(both.reshape(8, 192, 256), "ctx")
        (dn,) = run(k_qkv_back, [dt, wide], dq, arrived, *w)
        arrived = exchange(dn.reshape(8, 24, 1024), "tp")
        keep = slot((1024, 256), bf16)
        (send,) = run(k_grad_attn, [keep, ((1024, 256), bf16)], who, normed, dt, db, att)
        return arrived, (keep, swap(send))

    def grads_mlp(n, dpre, dm, hid):
        keep = slot((1024, 512), bf16)
        (send,) = run(k_grad_mlp, [keep, ((1024, 512), bf16)], who, n, dpre, dm, hid)
        return keep, send

    def to_rows(x):
        return exchange(x, "tp").reshape(192, 1024)

    normed0, q0, dm1 = rows192(1024), rows192(128), rows192(1024)
    (kv,) = run(k_first, [normed0, q0, ((8, 192, 256), bf16)], x_all, mods[0], *wa0)
    wa0 = sa[0]
    run(k_gate_rows, [dm1], cot_all, mods[1])
    kept0, arrived = attn_forward(q0, kv, wa0)
    br0, mid0 = rows24(), rows24()
    (n2,) = run(k_mid, [br0, mid0, bc], arrived, x0, mods[0])
    n2 = to_rows(n2)
    w0_other = swap(w0)
    wm0 = [Half(c, w0, w0_other, 1024, 1024, 0, 512, sm[0][c]) for c in range(2)]
    n2_0, hid0 = rows192(1024), rows192(512)
    (out,) = run(k_mlp, [hid0, wide], Save(n2, n2_0), *wm0)
    wm0 = sm[0]
    arrived = exchange(out.reshape(8, 24, 1024), "tp")
    mlp0, x1 = rows24(), rows24()
    (n1,) = run(k_next, [mlp0, x1, bc], arrived, mid0, mods[0], mods[1])

    w1 = lax.all_gather(w1, "ctx", axis=0, tiled=True)
    n1, w1 = lax.optimization_barrier((n1, w1))
    n1 = to_rows(n1)
    w1_other = swap(w1)
    wa1 = [Half(c, w1, w1_other, 1024, 1024, 0, 256, sa[1][c]) for c in range(2)]
    wm1 = [Half(c, w1, w1_other, 1024, 1024, 256, 512, sm[1][c]) for c in range(2)]
    normed1, q1 = rows192(1024), rows192(128)
    (kv,) = run(k_qkv, [q1, ((8, 192, 256), bf16)], Save(n1, normed1), *wa1)
    wa1 = sa[1]
    kept1, arrived = attn_forward(q1, kv, wa1)
    br1, mid1 = rows24(), rows24()
    (n2,) = run(k_mid, [br1, mid1, bc], arrived, x1, mods[1])
    n2 = to_rows(n2)
    n2_1, hid1, dpre1 = rows192(1024), rows192(512), rows192(512)
    (both,) = run(
        k_mlp_both, [hid1, dpre1, ((8, 2, 24, 1024), bf16)], Save(n2, n2_1), *wm1, dm1
    )
    arrived = exchange(both, "tp")
    res1, dmid1, dmod1a = rows24(), rows24(), rows24(12)
    (db,) = run(k_last, [res1, dmid1, dmod1a, bc], arrived, mid1, br1, cot, mods[1])
    gm1, send = grads_mlp(n2_1, dpre1, dm1, hid1)
    gm1 = gm1, swap(send)

    arrived, ga1 = attn_back(kept1, normed1, to_rows(db), wa1)
    dx1, dmod1b = rows24(), rows24(6)
    (dm,) = run(k_back_one, [dx1, dmod1b, bc], arrived, x1, dmid1, mods[1], mods[0])
    (mixed,) = run(k_grad_sum, [((1024, 768), bf16)], *gm1, *ga1)
    mixed = lax.psum_scatter(mixed, "ctx", tiled=True)
    dm = to_rows(dm)

    dm0, dpre0 = rows192(1024), rows192(512)
    (dn,) = run(k_mlp_back, [dpre0, wide], n2_0, *wm0, Save(dm, dm0))
    arrived = exchange(dn.reshape(8, 24, 1024), "tp")
    gm0, send = grads_mlp(n2_0, dpre0, dm0, hid0)
    dmid0, dmod0a = rows24(), rows24(12)
    (db,) = run(k_back_two, [dmid0, dmod0a, bc], arrived, mid0, br0, dx1, mlp0, mods[0])
    db, send = lax.optimization_barrier((db, send))
    (mixed0,) = run(k_grad_sum, [((1024, 512), bf16)], gm0, swap(send))
    mixed0 = lax.psum_scatter(mixed0, "ctx", tiled=True)
    arrived, ga0 = attn_back(kept0, normed0, to_rows(db), wa0)
    arrived, mixed = lax.optimization_barrier((arrived, mixed))
    keep, send = run(
        k_back_first, [((48, 1024), f32)] * 2,
        who, arrived, x0, dmid0, mods[0], dmod0a, dmod1a, dmod1b, res1,
    )

    (tail,) = run(k_tail_tp, [((8, 72, 1024), bf16)], who, keep, swap(send))
    tail = exchange(tail, "tp")
    tail, gm0 = lax.optimization_barrier((tail, mixed0))
    (tail_ctx,) = run(k_tail_ctx, [((8, 160, 256), bf16)], tail, *ga0)
    tail_ctx = exchange(tail_ctx, "ctx")
    ga0, grad_ada, spread = run(
        k_cond, [((128, 256), bf16), ((96, 1024), f32), ((64, 24, 128), bf16)],
        part_no, tail_ctx, cond_act, ada,
    )
    grad_act = exchange(spread, ("ctx", "tp"))
    tail, ga0, gm0 = lax.optimization_barrier((tail, ga0, gm0))
    (ends,) = run(k_ends, [((LAT, 128, 1024), f32)], tail)

    (send,) = run(k_final_send, [((128, 768), bf16)], who, gm0, mixed)
    grad_up, grad_down, grad_qkv, grad_out = run(
        k_final,
        [((128, 512), f32), ((512, 128), f32), ((3, 128, 128), f32), ((128, 128), f32)],
        who, gm0, mixed, swap(send), ga0, swap(ga0),
    )
    classes = jnp.arange(label_table.shape[0], dtype=jnp.int32)[:, None]
    match = [classes == labels[l] for l in range(LAT)]
    slope = jax.nn.sigmoid(condition)
    slope = slope * (1.0 + condition * (1.0 - slope))
    grad_act, ends, grad_up, grad_down, grad_qkv, grad_out, match, slope = lax.optimization_barrier(
        (grad_act, ends, grad_up, grad_down, grad_qkv, grad_out, match, slope)
    )
    grad_act = grad_act.astype(f32).sum(axis=0)
    grad_cond = (grad_act + swap(grad_act)).reshape(LAT, width) * slope
    grad_table = sum(jnp.where(match[l], grad_cond[l : l + 1], 0.0) for l in range(LAT))

    return (
        ends[None],
        grad_table,
        grad_ada.reshape(6, 16, width).transpose(2, 0, 1)[None],
        grad_qkv.transpose(1, 0, 2)[None],
        grad_out[None],
        grad_up[None],
        grad_down[None],
    )


def solution(mesh):
    return jax.shard_map(
        body,
        mesh=mesh,
        in_specs=(
            P(None, "ctx", None),
            P(None, "ctx", None),
            P(),
            P(),
            P(),
            P("pipe", None, None, ("ctx", "tp")),
            P("pipe", "ctx", None, "tp"),
            P("pipe", "tp", "ctx"),
            P("pipe", "ctx", "tp"),
            P("pipe", "tp", "ctx"),
        ),
        out_specs=(
            P("pipe", None, "ctx", None),
            P(),
            P("pipe", None, None, ("ctx", "tp")),
            P("pipe", "ctx", None, "tp"),
            P("pipe", "tp", "ctx"),
            P("pipe", "ctx", "tp"),
            P("pipe", "tp", "ctx"),
        ),
        check_vma=False,
    )
```

```python
import math

import jax
import jax.numpy as jnp
from jax import lax
from jax.experimental import pallas as pl
from jax.experimental.pallas import tpu as pltpu
from jax.sharding import PartitionSpec as P


LAT = 3
HEAD = 64
EPS = 1e-06
GELU_C = math.sqrt(2.0 / math.pi)
GELU_A = 0.044715
STORE_ROWS = 34048

f32 = jnp.float32
bf16 = jnp.bfloat16


def sds(shape, dtype):
    return jax.ShapeDtypeStruct(shape, dtype)


def up16(n):
    return -(-n // 16) * 16


class Slot:
    def __init__(self, row, shape, dtype):
        self.row, self.shape, self.dtype = row, shape, dtype
        self.rows = up16(shape[0]) * (2 if dtype == f32 else 1)

    def of(self, ref):
        return ref.at[pl.ds(self.row, self.rows), pl.ds(0, self.shape[1])]


class Store:
    def __init__(self):
        self.array, self.next = None, 0

    def slot(self, shape, dtype):
        s = Slot(self.next, shape, dtype)
        self.next += s.rows
        assert self.next <= STORE_ROWS
        return s


class Save:
    def __init__(self, array, slot):
        self.array, self.slot = array, slot


class Near:
    def __init__(self, array):
        self.array = array


class Half:
    def __init__(self, core, own, other, block, rows, at, width, slot):
        self.core, self.own, self.other = core, own, other
        self.block, self.rows, self.at, self.width, self.slot = block, rows, at, width, slot


class Held:
    def __init__(self, ref, wait, shape, dtype):
        self.ref, self.wait, self.shape, self.dtype = ref, wait, shape, dtype

    def ready(self):
        if self.wait is not None:
            self.wait()
            self.wait = None

    def __getitem__(self, at):
        self.ready()
        if self.dtype != f32 or self.ref.dtype == f32:
            return self.ref[at]
        n = self.shape[0]
        low = up16(n)
        return self.ref[:n].astype(f32) + self.ref[low : low + n].astype(f32)


class Kept:
    def __init__(self, ref, copy, shape, dtype):
        self.ref, self.copy, self.shape, self.dtype, self.gone = ref, copy, shape, dtype, False

    def send(self):
        if not self.gone:
            self.copy.start()
            self.gone = True

    def __setitem__(self, at, v):
        if self.dtype == f32:
            n = self.shape[0]
            low = up16(n)
            high = v.astype(bf16)
            self.ref[:n] = high
            self.ref[low : low + n] = (v - high.astype(f32)).astype(bf16)
            self.send()
        else:
            self.ref[at] = v
            if at is Ellipsis:
                self.send()


def ready(*refs):
    for r in refs:
        if isinstance(r, Held):
            r.ready()


def call(store, kernel, outs, *args, alone=False):
    vmem = pl.BlockSpec(memory_space=pltpu.VMEM)
    smem = pl.BlockSpec(memory_space=pltpu.SMEM)
    far = pl.BlockSpec(memory_space=pltpu.HBM)
    uses = any(isinstance(a, (Slot, Save, Half)) for a in args) or any(
        isinstance(o, Slot) for o in outs
    )
    flat, in_specs, plan, scratch = [], [], [], []

    def hold(shape, dtype):
        scratch.append(pltpu.VMEM(shape, dtype))
        return len(scratch) - 1

    for a in args:
        if isinstance(a, Slot):
            plan.append(("slot", a, hold((a.rows, a.shape[1]), bf16)))
        elif isinstance(a, Near):
            plan.append(("near", len(flat), hold(a.array.shape, a.array.dtype)))
            flat.append(a.array)
            in_specs.append(far)
        elif isinstance(a, Half):
            plan.append(("half", len(flat), hold(a.slot.shape, bf16), a))
            flat += [a.own, a.other]
            in_specs += [far, far]
        else:
            v = a.array if isinstance(a, Save) else a
            plan.append(("here", len(flat), a))
            flat.append(v)
            in_specs.append(smem if v.dtype == jnp.int32 else vmem)
    out_shape, out_specs, out_plan = [], [], []
    for o in outs:
        if isinstance(o, Slot):
            out_plan.append((o, hold((o.rows, o.shape[1]), bf16)))
        elif alone:
            out_plan.append((len(out_shape), hold(*o)))
            out_shape.append(sds(*o))
            out_specs.append(far)
        else:
            out_plan.append((None, len(out_shape)))
            out_shape.append(sds(*o))
            out_specs.append(vmem)
    n_args, n_out, n_hold = len(flat), len(out_shape), len(scratch)
    n_saves = sum(isinstance(a, (Save, Half)) for a in args)
    alias = {}
    if uses:
        if store.array is not None:
            flat.append(store.array)
            in_specs.append(far)
            alias = {len(flat) - 1: n_out}
        out_shape.append(sds((STORE_ROWS, 1024), bf16))
        out_specs.append(far)
    n_in = len(flat)
    n_sems = n_hold + n_saves

    def wrapped(*refs):
        ins, results = refs[:n_in], refs[n_in : n_in + len(out_shape)]
        holds = refs[n_in + len(out_shape) :]
        sems = holds[n_hold] if n_sems else None
        big = results[n_out] if uses else None
        given, leaving, late = [], [], n_hold
        for item in plan:
            if item[0] == "here":
                given.append(ins[item[1]])
                if isinstance(item[2], Save):
                    copy = pltpu.make_async_copy(ins[item[1]], item[2].slot.of(big), sems.at[late])
                    copy.start()
                    leaving.append(copy)
                    late += 1
                continue
            to, sem = holds[item[2]], sems.at[item[2]]
            if item[0] == "half":
                h = item[3]
                mine = lax.axis_index("pipe") == h.core
                for k in range(2):

                    @pl.when(mine if k == 0 else jnp.logical_not(mine))
                    def _(src=ins[item[1] + k]):
                        for c in range(h.slot.shape[0] // h.rows):
                            pltpu.make_async_copy(
                                src.at[pl.ds(c * h.block, h.rows), pl.ds(h.at, h.width)],
                                to.at[pl.ds(c * h.rows, h.rows)],
                                sem,
                            ).start()

                whole = pltpu.make_async_copy(to, to, sem)
                out = pltpu.make_async_copy(to, h.slot.of(big), sems.at[late])
                late += 1
                leaving.append(out)

                def arrive(whole=whole, out=out):
                    whole.wait()
                    out.start()

                given.append(Held(to, arrive, h.slot.shape, bf16))
                continue
            if item[0] == "slot":
                copy = pltpu.make_async_copy(item[1].of(big), to, sem)
                shape, dtype = item[1].shape, item[1].dtype
            else:
                copy = pltpu.make_async_copy(ins[item[1]], to, sem)
                shape, dtype = to.shape, to.dtype
            copy.start()
            given.append(Held(to, copy.wait, shape, dtype))
        for slot, at in out_plan:
            if slot is None:
                given.append(results[at])
            else:
                if isinstance(slot, Slot):
                    copy = pltpu.make_async_copy(holds[at], slot.of(big), sems.at[at])
                    kept = Kept(holds[at], copy, slot.shape, slot.dtype)
                else:
                    copy = pltpu.make_async_copy(holds[at], results[slot], sems.at[at])
                    kept = Kept(holds[at], copy, None, None)
                leaving.append(copy)
                given.append(kept)
        kernel(*given)
        ready(*given)
        for g in given:
            if isinstance(g, Kept):
                g.send()
        for copy in leaving:
            copy.wait()

    got = pl.pallas_call(
        wrapped,
        out_shape=tuple(out_shape),
        in_specs=in_specs,
        out_specs=tuple(out_specs),
        scratch_shapes=scratch + ([pltpu.SemaphoreType.DMA((n_sems,))] if n_sems else []),
        input_output_aliases=alias,
        compiler_params=pltpu.CompilerParams(vmem_limit_bytes=(60 if alone else 24) * 1024 * 1024),
    )(*flat)
    if uses:
        store.array = got[n_out]
    return got[:n_out]


def mm(a, b):
    return lax.dot_general(a, b, (((1,), (0,)), ((), ())), preferred_element_type=f32)


def mm_nt(a, b):
    return lax.dot_general(a, b, (((1,), (1,)), ((), ())), preferred_element_type=f32)


def mm_tn(a, b):
    return lax.dot_general(a, b, (((0,), (0,)), ((), ())), preferred_element_type=f32)


def part(mod, k):
    return jnp.concatenate(
        [jnp.broadcast_to(mod[3 * k + l : 3 * k + l + 1, :], (8, mod.shape[1])) for l in range(LAT)],
        axis=0,
    )


def centred(x):
    c = x - jnp.mean(x, axis=-1, keepdims=True)
    r = lax.rsqrt(jnp.mean(c * c, axis=-1, keepdims=True) + EPS)
    return c * r, r


def norm_back(x, dy, scale):
    xh, r = centred(x)
    g = dy * (1.0 + scale)
    dx = r * (
        g - jnp.mean(g, axis=-1, keepdims=True) - xh * jnp.mean(g * xh, axis=-1, keepdims=True)
    )
    return dx, dy, dy * xh


def row_sums(*vs):
    return jnp.concatenate(
        [jnp.sum(v[8 * l : 8 * l + 8], axis=0, keepdims=True) for v in vs for l in range(LAT)], axis=0
    )


def summed(ref, *at):
    total = ref[(0, *at)].astype(f32)
    for j in range(1, 8):
        total = total + ref[(j, *at)].astype(f32)
    return total


def to_all(ref, v):
    for j in range(8):
        ref[j] = v


def by_latent(v):
    v = v.reshape(8, LAT, 8, v.shape[-1])
    return [v[:, l].reshape(64, v.shape[-1]) for l in range(LAT)]


def rows_of(v):
    return v.reshape(-1, v.shape[-1])


def by_part(vs):
    w = vs[0].shape[-1]
    return jnp.stack([v.reshape(8, 8, w) for v in vs], axis=1).reshape(192, w)


def gelu_parts(x):
    t = jnp.tanh(GELU_C * (x + GELU_A * (x * x * x)))
    return t


def k_halves(p_ref, wq_ref, wo_ref, up_ref, down_ref, keep_ref, send_ref):
    ready(wq_ref, wo_ref, up_ref, down_ref)

    a = jnp.concatenate([wq_ref[0], wq_ref[1], up_ref[...]], axis=1).astype(f32)
    wo, down = wo_ref[...].astype(f32).T, down_ref[...].astype(f32).T
    b = jnp.concatenate([wq_ref[2].astype(f32), wo, down], axis=1)
    first = p_ref[0] == 0
    send_ref[...] = jnp.where(first, b, a).astype(bf16)
    keep_ref[...] = jnp.where(first, a, b).astype(bf16)


def k_pack(
    p_ref, t_ref, lab_ref, table_ref, sinus_ref, ada_ref, keep_ref, got_ref,
    o_ref, w0_ref, w1_ref, cond_ref, act_ref,
):
    first = p_ref[0] == 0
    keep, got = keep_ref[...].astype(f32), got_ref[...].astype(f32)
    w0 = jnp.where(first, keep, got).astype(bf16)
    w0_ref[...] = w0[:, 256:]
    w1_ref[...] = jnp.where(first, got, keep).astype(bf16)
    row = lax.broadcasted_iota(jnp.int32, (8, table_ref.shape[0]), 0)
    col = lax.broadcasted_iota(jnp.int32, (8, table_ref.shape[0]), 1)
    label = jnp.where(row == 0, lab_ref[0], jnp.where(row == 1, lab_ref[1], lab_ref[2]))
    cond = mm(jnp.where(col == label, 1.0, 0.0).astype(bf16), table_ref[...])[:LAT] + sinus_ref[...]
    cond_ref[...] = cond
    act = (cond / (1.0 + jnp.exp(-cond))).astype(bf16)
    act_ref[...] = act
    row = lax.broadcasted_iota(jnp.int32, (96, 768), 0)
    lane = lax.broadcasted_iota(jnp.int32, (96, 768), 1)
    to = 128 * (row // 16) + row % 16 + 16 * t_ref[0]
    place = jnp.where(lane == to, 1.0, 0.0).astype(bf16)
    mod = mm(mm_nt(act, ada_ref[...]).astype(bf16), place)
    mod = jnp.concatenate([mod[:, 128 * k : 128 * k + 128] for k in range(6)], axis=0)
    mod = jnp.concatenate([mod, jnp.zeros((14, 128), f32)], axis=0)
    mod = jnp.concatenate([mod, jnp.zeros((32, 128), f32)], axis=1).astype(bf16)
    for j in range(8):
        o_ref[j, :128] = w0[:, :256]
        o_ref[j, 128:] = mod


def k_spread(r_ref, o_ref):
    for c in range(8):
        v = r_ref[c, 128:, :128][:24]
        for j in range(8):
            o_ref[j, c] = v


def k_mods(r_ref, o_ref):
    for c in range(8):
        o_ref[:, 128 * c : 128 * c + 128] = summed(r_ref, c).astype(bf16)


def k_two_layers(p_ref, own_ref, other_ref, a_ref, b_ref):
    own, other, first = own_ref[...].astype(f32), other_ref[...].astype(f32), p_ref[0] == 0
    a_ref[...] = jnp.where(first, own, other).astype(bf16)
    b_ref[...] = jnp.where(first, other, own).astype(bf16)


def put_qkv(y, q_ref, kv_ref):
    y = jnp.concatenate(by_latent(y), axis=0).astype(bf16)
    q_ref[...] = y[:, :128]
    to_all(kv_ref, y[:, 128:])


def triple(n, wa_ref, wb_ref):
    a = mm(n, rows_of(wa_ref[...]))
    return jnp.concatenate([a, mm(n, rows_of(wb_ref[...])[:, :128])], axis=1)


def k_rows(p_ref, t_ref, x_ref, c_ref, x_all_ref, x_own_ref, c_all_ref, c_own_ref):
    start = pl.multiple_of(64 * p_ref[0], 64)
    few = pl.multiple_of(64 * p_ref[0] + 8 * t_ref[0], 8)
    ready(x_ref, c_ref)
    for ref, all_ref, own_ref in ((x_ref.ref, x_all_ref, x_own_ref), (c_ref.ref, c_all_ref, c_own_ref)):
        blocks = [ref[l, pl.ds(start, 64), :] for l in range(LAT)]
        all_ref[...] = jnp.concatenate(
            [b[8 * j : 8 * j + 8] for j in range(8) for b in blocks], axis=0
        )
        own_ref[...] = jnp.concatenate([ref[l, pl.ds(few, 8), :] for l in range(LAT)], axis=0)


def k_first(x_ref, mod_ref, wa_ref, wb_ref, n_ref, q_ref, kv_ref):
    mod = mod_ref[...].astype(f32)
    shift, scale = part(mod, 0), 1.0 + part(mod, 1)
    x = x_ref[...]
    rows = [centred(x[24 * j : 24 * j + 24])[0] * scale + shift for j in range(8)]
    n = jnp.concatenate(rows, axis=0).astype(bf16)
    n_ref[...] = n
    put_qkv(triple(n, wa_ref, wb_ref), q_ref, kv_ref)


def k_qkv(n_ref, wa_ref, wb_ref, q_ref, kv_ref):
    put_qkv(triple(n_ref[...], wa_ref, wb_ref), q_ref, kv_ref)


def head_rows(v):
    lane = lax.broadcasted_iota(jnp.int32, v.shape, 1)
    zero = jnp.zeros_like(v)
    return jnp.concatenate(
        [jnp.where(lane < HEAD, v, zero), jnp.where(lane < HEAD, zero, v)], axis=0
    )


def head_lanes(v):
    lane = lax.broadcasted_iota(jnp.int32, (64, 128), 1)
    return jnp.where(lane < HEAD, v[:64], v[64:])


def keys_values(a_ref, b_ref, l):
    at = [64 * (LAT * c + l) for c in range(8)]
    kv = jnp.concatenate([r[i : i + 64] for r in (a_ref, b_ref) for i in at], axis=0)
    return kv[:, :128], kv[:, 128:]


def soft(qs, k):
    s = mm_nt(k, qs) * 0.125
    e = jnp.exp(s - jnp.max(s, axis=0, keepdims=True))
    return e * (1.0 / jnp.sum(e, axis=0, keepdims=True))


def k_attn(q_ref, a_ref, b_ref, w_ref, att_ref, o_ref):
    outs = []
    for l in range(LAT):
        k, v = keys_values(a_ref, b_ref, l)
        probs = soft(head_rows(q_ref[64 * l : 64 * l + 64].astype(f32)).astype(bf16), k)
        outs.append(head_lanes(mm_tn(probs.astype(bf16), v)))
    att = by_part(outs).astype(bf16)
    att_ref[...] = att
    o_ref[...] = mm_nt(att, rows_of(w_ref[...])[:, 128:]).astype(bf16)


def k_attn_back(q_ref, a_ref, b_ref, w_ref, db_ref, dq_ref, da_ref, dp_ref):
    datt = by_latent(mm(db_ref[...], rows_of(w_ref[...])[:, 128:]))
    for l in range(LAT):
        k, v = keys_values(a_ref, b_ref, l)
        qs = head_rows(q_ref[64 * l : 64 * l + 64].astype(f32)).astype(bf16)
        do = head_rows(datt[l]).astype(bf16)
        probs = soft(qs, k)
        dprobs = mm_nt(v, do)
        dv = mm(probs.astype(bf16), do)
        ds = probs * (dprobs - jnp.sum(probs * dprobs, axis=0, keepdims=True))
        ds = ds.astype(bf16)
        dk = mm(ds, qs) * 0.125
        dq_ref[64 * l : 64 * l + 64] = (head_lanes(mm_tn(ds, k)) * 0.125).astype(bf16)
        dkv = jnp.concatenate([dk, dv], axis=1).astype(bf16)
        for c in range(8):
            at = 64 * (LAT * c + l)
            da_ref[at : at + 64] = dkv[64 * c : 64 * c + 64]
            dp_ref[at : at + 64] = dkv[512 + 64 * c : 512 + 64 * c + 64]


def k_pair_sum(a_ref, b_ref, o_ref):
    o_ref[...] = (a_ref[...].astype(f32) + b_ref[...].astype(f32)).astype(bf16)


def k_qkv_back(dq_ref, r_ref, wa_ref, wb_ref, dt_ref, o_ref):
    dt = jnp.concatenate([dq_ref[...].astype(f32), summed(r_ref)], axis=1)
    dt = by_part([dt[64 * l : 64 * l + 64] for l in range(LAT)]).astype(bf16)
    dt_ref[...] = dt
    back = mm_nt(dt[:, :256], rows_of(wa_ref[...])) + mm_nt(dt[:, 256:], rows_of(wb_ref[...])[:, :128])
    o_ref[...] = back.astype(bf16)


def k_mid(r_ref, x_ref, mod_ref, br_ref, mid_ref, o_ref):
    mod = mod_ref[...].astype(f32)
    branch = summed(r_ref)
    mid = x_ref[...] + part(mod, 2) * branch
    br_ref[...] = branch
    mid_ref[...] = mid
    xh, _ = centred(mid)
    to_all(o_ref, (xh * (1.0 + part(mod, 4)) + part(mod, 3)).astype(bf16))


def k_mlp(n_ref, up_ref, down_ref, hid_ref, o_ref):
    pre = mm(n_ref[...], rows_of(up_ref[...]))
    hid = (0.5 * pre * (1.0 + gelu_parts(pre))).astype(bf16)
    hid_ref[...] = hid
    o_ref[...] = mm_nt(hid, rows_of(down_ref[...])).astype(bf16)


def gelu_slope(pre, t):
    inner = GELU_C * (1.0 + 3.0 * GELU_A * pre * pre)
    return 0.5 * (1.0 + t) + 0.5 * pre * (1.0 - t * t) * inner


def k_mlp_both(n_ref, up_ref, down_ref, dm_ref, hid_ref, dpre_ref, o_ref):
    pre = mm(n_ref[...], rows_of(up_ref[...]))
    t = gelu_parts(pre)
    hid = (0.5 * pre * (1.0 + t)).astype(bf16)
    hid_ref[...] = hid
    out = mm_nt(hid, rows_of(down_ref[...])).astype(bf16)
    dhid = mm(dm_ref[...], rows_of(down_ref[...]))
    dpre = (dhid * gelu_slope(pre, t)).astype(bf16)
    dpre_ref[...] = dpre
    back = mm_nt(dpre, rows_of(up_ref[...])).astype(bf16)
    for j in range(8):
        o_ref[j, 0] = out[24 * j : 24 * j + 24]
        o_ref[j, 1] = back[24 * j : 24 * j + 24]


def k_mlp_back(n_ref, up_ref, down_ref, dm_ref, dpre_ref, o_ref):
    pre = mm(n_ref[...], rows_of(up_ref[...]))
    dhid = mm(dm_ref[...], rows_of(down_ref[...]))
    dpre = (dhid * gelu_slope(pre, gelu_parts(pre))).astype(bf16)
    dpre_ref[...] = dpre
    o_ref[...] = mm_nt(dpre, rows_of(up_ref[...])).astype(bf16)


def k_gate_rows(c_ref, mod_ref, o_ref):
    gate = part(mod_ref[...].astype(f32), 5)
    c = c_ref[...]
    rows = [gate * c[24 * j : 24 * j + 24] for j in range(8)]
    o_ref[...] = jnp.concatenate(rows, axis=0).astype(bf16)


def k_next(r_ref, mid_ref, mod_ref, mod_next_ref, mlp_ref, x_ref, o_ref):
    mod, mod_next = mod_ref[...].astype(f32), mod_next_ref[...].astype(f32)
    mlp = summed(r_ref)
    mlp_ref[...] = mlp
    x = mid_ref[...] + part(mod, 5) * mlp
    x_ref[...] = x
    xh, _ = centred(x)
    to_all(o_ref, (xh * (1.0 + part(mod_next, 1)) + part(mod_next, 0)).astype(bf16))


def back_two(mod, mid, branch, dy, dn, mlp, dmid_ref, dmod_ref, o_ref):
    dx, ds, dc = norm_back(mid, dn, part(mod, 4))
    dmid = dy + dx
    dmid_ref[...] = dmid
    to_all(o_ref, (part(mod, 2) * dmid).astype(bf16))
    dmod_ref[...] = row_sums(dmid * branch, ds, dc, dy * mlp)


def k_last(r_ref, mid_ref, br_ref, dy_ref, mod_ref, res_ref, dmid_ref, dmod_ref, o_ref):
    mod = mod_ref[...].astype(f32)
    mlp, dn = summed(r_ref, 0), summed(r_ref, 1)
    mid = mid_ref[...]
    res_ref[...] = mid + part(mod, 5) * mlp
    back_two(mod, mid, br_ref[...], dy_ref[...], dn, mlp, dmid_ref, dmod_ref, o_ref)


def k_back_two(r_ref, mid_ref, br_ref, dy_ref, mlp_ref, mod_ref, dmid_ref, dmod_ref, o_ref):
    mod = mod_ref[...].astype(f32)
    back_two(
        mod, mid_ref[...], br_ref[...], dy_ref[...], summed(r_ref), mlp_ref[...],
        dmid_ref, dmod_ref, o_ref,
    )


def k_back_one(r_ref, x_ref, dmid_ref, mod_ref, mod_before_ref, dx_ref, dmod_ref, o_ref):
    dx, ds, dc = norm_back(x_ref[...], summed(r_ref), part(mod_ref[...].astype(f32), 1))
    dx = dmid_ref[...] + dx
    dx_ref[...] = dx
    dmod_ref[...] = row_sums(ds, dc)
    to_all(o_ref, (part(mod_before_ref[...].astype(f32), 5) * dx).astype(bf16))


def k_early(p_ref, d0_ref, d1a_ref, d1b_ref, keep_ref, send_ref):
    first = p_ref[0] == 0
    none = jnp.zeros((6, keep_ref.shape[1]), f32)
    d0 = jnp.concatenate([none, d0_ref[...]], axis=0)
    d1 = jnp.concatenate([d1b_ref[...], d1a_ref[...]], axis=0)
    keep_ref[...] = jnp.where(first, d0, d1)
    send_ref[...] = jnp.where(first, d1, d0)


def k_qkv_back_first(dq_ref, r_ref, wa_ref, wb_ref, x_ref, keep_ref, got_ref, dt_ref, o_ref):
    dt = jnp.concatenate([dq_ref[...].astype(f32), summed(r_ref)], axis=1)
    dt = by_part([dt[64 * l : 64 * l + 64] for l in range(LAT)]).astype(bf16)
    dt_ref[...] = dt
    back = mm_nt(dt[:, :256], rows_of(wa_ref[...])) + mm_nt(dt[:, 256:], rows_of(wb_ref[...])[:, :128])
    x = x_ref[...]
    ds = jnp.zeros((24, x.shape[1]), f32)
    dc = jnp.zeros((24, x.shape[1]), f32)
    for j in range(8):
        dn = back[24 * j : 24 * j + 24]
        ds = ds + dn
        dc = dc + dn * centred(x[24 * j : 24 * j + 24])[0]
    sums = jnp.concatenate([row_sums(ds, dc), keep_ref[...] + got_ref[...]], axis=0)
    for j in range(8):
        o_ref[j] = jnp.concatenate([back[24 * j : 24 * j + 24], sums], axis=0).astype(bf16)


def rows_sum(r_ref, at, n):
    total = r_ref[0].astype(f32)[at : at + n]
    for j in range(1, 8):
        total = total + r_ref[j].astype(f32)[at : at + n]
    return total


def k_back_first(p_ref, r_ref, x_ref, dmid_ref, mod_ref, res_ref, keep_ref, send_ref):
    first = p_ref[0] == 0
    dn = rows_sum(r_ref, 0, 24)
    dx, _, _ = norm_back(x_ref[...], dn, part(mod_ref[...].astype(f32), 1))
    dx = dmid_ref[...] + dx
    res = res_ref[...]
    keep_ref[...] = jnp.where(first, dx, res)
    send_ref[...] = jnp.where(first, res, dx)


def k_tail_ctx(r_ref, a_ref, b_ref, o_ref):
    total = rows_sum(r_ref, 24, 24)
    total = jnp.concatenate([total, jnp.zeros((8, total.shape[1]), f32)], axis=0).astype(bf16)
    none = jnp.zeros((32, 128), bf16)
    for c in range(8):
        at = slice(128 * c, 128 * c + 128)
        o_ref[c, :128, :] = (a_ref[at].astype(f32) + b_ref[at].astype(f32)).astype(bf16)
        o_ref[c, 128:, :128] = total[:, at]
        o_ref[c, 128:, 128:] = none


def k_ends(r_ref, o_ref):
    for j in range(8):
        v = r_ref[j].astype(f32)
        for half in range(2):
            for l in range(LAT):
                at = 64 * half + 8 * j
                o_ref[l, at : at + 8, :] = v[24 * half + 8 * l : 24 * half + 8 * l + 8]


def k_cond(
    p_ref, t_ref, r_ref, other_ref, act_ref, ada_ref, keep_ref, got_ref, g_ref, ada_grad_ref, o_ref
):
    first = p_ref[0] == 0
    total = summed(r_ref)
    d = total[128:, :128]
    late = jnp.where(first, d[:6] + summed(other_ref)[:6], 0.0)
    d = jnp.concatenate([d[6:12] + late, d[12:24], jnp.zeros((14, 128), f32)], axis=0)
    lane = lax.broadcasted_iota(jnp.int32, (128, 16), 0)
    col = lax.broadcasted_iota(jnp.int32, (128, 16), 1)
    pick = jnp.where(lane == col + 16 * t_ref[0], 1.0, 0.0).astype(bf16)
    d = mm(d.astype(bf16), pick)
    act = act_ref[...]
    c = jnp.zeros(act.shape, f32)
    for k in range(6):
        dk = d[3 * k : 3 * k + 3].astype(bf16)
        ada_grad_ref[16 * k : 16 * k + 16, :] = mm_tn(dk, act)
        c = c + mm(dk, ada_ref[16 * k : 16 * k + 16, :])
    keep, got = keep_ref[...], got_ref[...]
    v = [jnp.where(first, keep, got), jnp.where(first, got, keep), c, jnp.zeros((13, c.shape[1]), f32)]
    to_all(o_ref, jnp.concatenate(v, axis=0).astype(bf16))
    g_ref[...] = total[:128].astype(bf16)


def k_cond_tp(r_ref, o_ref):
    to_all(o_ref, rows_sum(r_ref, 48, 8))


def k_final_send(p_ref, m0_ref, m1_ref, o_ref):
    m0, m1 = m0_ref[...].astype(f32), m1_ref[...].astype(f32)
    o_ref[:, :512] = jnp.where(p_ref[0] == 0, m1[:, :512], m0).astype(bf16)
    o_ref[:, 512:] = m1[:, 512:].astype(bf16)


def k_final(p_ref, m0_ref, m1_ref, a_ref, g_ref, b_ref, up_ref, down_ref, qkv_ref, out_ref):
    first = p_ref[0] == 0
    m0, m1, a = (r[...].astype(f32) for r in (m0_ref, m1_ref, a_ref))
    g, b = g_ref[...].astype(f32), b_ref[...].astype(f32)
    up_ref[...] = jnp.where(first, m0, a[:, :512])
    down_ref[...] = jnp.where(first, a[:, :512], m1[:, :512]).T
    qk = jnp.where(first, g, a[:, 512:])
    vo = jnp.where(first, b, m1[:, 512:])
    qkv_ref[0], qkv_ref[1], qkv_ref[2] = qk[:, :128], qk[:, 128:], vo[:, :128]
    out_ref[...] = vo[:, 128:].T


def k_grad_mlp(p_ref, n_ref, dpre_ref, dm_ref, hid_ref, keep_ref, send_ref):
    first = p_ref[0] == 0
    n, dm = n_ref[...], dm_ref[...]
    dpre, hid = dpre_ref[...], hid_ref[...]

    def pick(a, b):
        return jnp.where(first, a.astype(f32), b.astype(f32)).astype(bf16)

    send_ref[...] = mm_tn(pick(dm, n), pick(hid, dpre)).astype(bf16)
    keep_ref[...] = mm_tn(pick(n, dm), pick(dpre, hid)).astype(bf16)


def k_grad_attn(p_ref, n_ref, dt_ref, db_ref, att_ref, keep_ref, send_ref):
    first = p_ref[0] == 0
    n, dt = n_ref[...], dt_ref[...]
    qk = mm_tn(n, dt[:, :256])
    vo = jnp.concatenate([mm_tn(n, dt[:, 256:]), mm_tn(db_ref[...], att_ref[...])], axis=1)
    send_ref[...] = jnp.where(first, vo, qk).astype(bf16)
    keep_ref[...] = jnp.where(first, qk, vo).astype(bf16)


def k_grad_sum(*refs):
    o_ref, at = refs[-1], 0
    for keep, got in zip(refs[0:-1:2], refs[1:-1:2]):
        v = (keep[...].astype(f32) + got[...].astype(f32)).astype(bf16)
        o_ref[:, at : at + v.shape[1]] = v
        at += v.shape[1]


def exchange(x, axis):
    return lax.all_to_all(x, axis, 0, 0, tiled=True)


def swap(x):
    return lax.ppermute(x, "pipe", [(0, 1), (1, 0)])


def body(latents, cotangent, labels, steps, label_table, w_ada, w_qkv, w_out, w_up, w_down):
    p, t = lax.axis_index("pipe"), lax.axis_index("tp")
    who, part_no = p.astype(jnp.int32).reshape(1), t.astype(jnp.int32).reshape(1)
    width = latents.shape[2]

    store = Store()
    slot = store.slot

    def run(kernel, outs, *args, alone=False):
        return call(store, kernel, outs, *args, alone=alone)

    keep, send = run(
        k_halves, [((128, 768), bf16)] * 2,
        who, Near(w_qkv[0].transpose(1, 0, 2)), Near(w_out[0]), Near(w_up[0]), Near(w_down[0]),
        alone=True,
    )
    half = width // 2
    freq = jnp.exp(-math.log(10000.0) * jnp.arange(half, dtype=f32) / half)
    angles = steps.astype(f32)[:, None] * freq[None, :]
    sinus = jnp.concatenate([jnp.cos(angles), jnp.sin(angles)], axis=1)
    ada = w_ada[0].transpose(1, 2, 0).reshape(96, width)
    packed, w0, w1, condition, cond_act = run(
        k_pack,
        [
            ((8, 160, 256), bf16), ((128, 512), bf16), ((128, 768), bf16),
            ((LAT, width), f32), ((LAT, width), bf16),
        ],
        who, part_no, labels, Near(label_table), Near(sinus), Near(ada), Near(keep), Near(swap(send)),
        alone=True,
    )
    w0 = lax.all_gather(w0, "ctx", axis=0, tiled=True)
    packed = exchange(packed, "ctx")
    packed, latents, cotangent = lax.optimization_barrier((packed, latents, cotangent))
    (spread,) = run(k_spread, [((8, 8, 24, 128), bf16)], packed)
    packed = packed.reshape(1280, 256)
    packed_other = swap(packed)
    sa = [[slot((1024, 256), bf16) for _ in range(2)] for _ in range(2)]
    sm = [[slot((1024, 512), bf16) for _ in range(2)] for _ in range(2)]
    wa0 = [Half(c, packed, packed_other, 160, 128, 0, 256, sa[0][c]) for c in range(2)]
    x_all, x0 = slot((192, 1024), f32), slot((24, 1024), f32)
    cot_all, cot = slot((192, 1024), f32), slot((24, 1024), f32)
    run(k_rows, [x_all, x0, cot_all, cot], who, part_no, Near(latents), Near(cotangent), alone=True)
    spread, store.array = lax.optimization_barrier((exchange(spread, "tp"), store.array))
    (mod_own,) = run(k_mods, [((24, 1024), bf16)], spread)
    mods = run(k_two_layers, [((24, 1024), bf16)] * 2, who, mod_own, swap(mod_own))

    bc = ((8, 24, 1024), bf16)
    wide = ((192, 1024), bf16)
    kv_all = ((1536, 256), bf16)

    def rows24(n=24):
        return slot((n, 1024), f32)

    def rows192(n):
        return slot((192, n), bf16)

    def attn_forward(q, kv, w):
        kv_a = exchange(kv, "ctx").reshape(1536, 256)
        kv_b = swap(kv_a)
        att, sa, sb = rows192(128), slot((1536, 256), bf16), slot((1536, 256), bf16)
        (branch,) = run(k_attn, [att, wide], q, Save(kv_a, sa), Save(kv_b, sb), w[1])
        return (q, sa, sb, att), exchange(branch.reshape(8, 24, 1024), "tp")

    def attn_back(kept, normed, dbranch, w, last=None):
        q, kv_a, kv_b, att = kept
        db, dq, dt = rows192(1024), rows192(128), rows192(384)
        da, dp = run(k_attn_back, [dq, kv_all, kv_all], q, kv_a, kv_b, w[1], Save(dbranch, db))
        (both,) = run(k_pair_sum, [kv_all], da, swap(dp))
        arrived = exchange(both.reshape(8, 192, 256), "ctx")
        if last is None:
            (dn,) = run(k_qkv_back, [dt, wide], dq, arrived, *w)
            dn = dn.reshape(8, 24, 1024)
        else:
            (dn,) = run(k_qkv_back_first, [dt, ((8, 48, 1024), bf16)], dq, arrived, *w, *last)
        arrived = exchange(dn, "tp")
        keep = slot((1024, 256), bf16)
        (send,) = run(k_grad_attn, [keep, ((1024, 256), bf16)], who, normed, dt, db, att)
        return arrived, (keep, swap(send))

    def grads_mlp(n, dpre, dm, hid):
        keep = slot((1024, 512), bf16)
        (send,) = run(k_grad_mlp, [keep, ((1024, 512), bf16)], who, n, dpre, dm, hid)
        return keep, send

    def to_rows(x):
        return exchange(x, "tp").reshape(192, 1024)

    normed0, q0, dm1 = rows192(1024), rows192(128), rows192(1024)
    (kv,) = run(k_first, [normed0, q0, ((8, 192, 256), bf16)], x_all, mods[0], *wa0)
    wa0 = sa[0]
    run(k_gate_rows, [dm1], cot_all, mods[1])
    kept0, arrived = attn_forward(q0, kv, wa0)
    br0, mid0 = rows24(), rows24()
    (n2,) = run(k_mid, [br0, mid0, bc], arrived, x0, mods[0])
    n2 = to_rows(n2)
    w0_other = swap(w0)
    wm0 = [Half(c, w0, w0_other, 1024, 1024, 0, 512, sm[0][c]) for c in range(2)]
    n2_0, hid0 = rows192(1024), rows192(512)
    (out,) = run(k_mlp, [hid0, wide], Save(n2, n2_0), *wm0)
    wm0 = sm[0]
    arrived = exchange(out.reshape(8, 24, 1024), "tp")
    mlp0, x1 = rows24(), rows24()
    (n1,) = run(k_next, [mlp0, x1, bc], arrived, mid0, mods[0], mods[1])

    w1 = lax.all_gather(w1, "ctx", axis=0, tiled=True)
    n1, w1 = lax.optimization_barrier((n1, w1))
    n1 = to_rows(n1)
    w1_other = swap(w1)
    wa1 = [Half(c, w1, w1_other, 1024, 1024, 0, 256, sa[1][c]) for c in range(2)]
    wm1 = [Half(c, w1, w1_other, 1024, 1024, 256, 512, sm[1][c]) for c in range(2)]
    normed1, q1 = rows192(1024), rows192(128)
    (kv,) = run(k_qkv, [q1, ((8, 192, 256), bf16)], Save(n1, normed1), *wa1)
    wa1 = sa[1]
    kept1, arrived = attn_forward(q1, kv, wa1)
    br1, mid1 = rows24(), rows24()
    (n2,) = run(k_mid, [br1, mid1, bc], arrived, x1, mods[1])
    n2 = to_rows(n2)
    n2_1, hid1, dpre1 = rows192(1024), rows192(512), rows192(512)
    (both,) = run(
        k_mlp_both, [hid1, dpre1, ((8, 2, 24, 1024), bf16)], Save(n2, n2_1), *wm1, dm1
    )
    arrived = exchange(both, "tp")
    res1, dmid1, dmod1a = rows24(), rows24(), rows24(12)
    (db,) = run(k_last, [res1, dmid1, dmod1a, bc], arrived, mid1, br1, cot, mods[1])
    gm1, send = grads_mlp(n2_1, dpre1, dm1, hid1)
    gm1 = gm1, swap(send)

    arrived, ga1 = attn_back(kept1, normed1, to_rows(db), wa1)
    dx1, dmod1b = rows24(), rows24(6)
    (dm,) = run(k_back_one, [dx1, dmod1b, bc], arrived, x1, dmid1, mods[1], mods[0])
    (mixed,) = run(k_grad_sum, [((1024, 768), bf16)], *gm1, *ga1)
    mixed = lax.psum_scatter(mixed, "ctx", tiled=True)
    dm = to_rows(dm)

    dm0, dpre0 = rows192(1024), rows192(512)
    (dn,) = run(k_mlp_back, [dpre0, wide], n2_0, *wm0, Save(dm, dm0))
    arrived = exchange(dn.reshape(8, 24, 1024), "tp")
    gm0, send = grads_mlp(n2_0, dpre0, dm0, hid0)
    dmid0, dmod0a = rows24(), rows24(12)
    (db,) = run(k_back_two, [dmid0, dmod0a, bc], arrived, mid0, br0, dx1, mlp0, mods[0])
    db, send = lax.optimization_barrier((db, send))
    (mixed0,) = run(k_grad_sum, [((1024, 512), bf16)], gm0, swap(send))
    mixed0 = lax.psum_scatter(mixed0, "ctx", tiled=True)
    keep, send = run(k_early, [((18, 1024), f32)] * 2, who, dmod0a, dmod1a, dmod1b)
    arrived, ga0 = attn_back(kept0, normed0, to_rows(db), wa0, (x_all, keep, swap(send)))
    arrived, mixed = lax.optimization_barrier((arrived, mixed))

    (tail_ctx,) = run(k_tail_ctx, [((8, 160, 256), bf16)], arrived, *ga0)
    keep, send = run(
        k_back_first, [((24, 1024), f32)] * 2, who, arrived, x0, dmid0, mods[0], res1
    )
    tail_ctx = exchange(tail_ctx, "ctx")
    ga0, grad_ada, tail = run(
        k_cond, [((128, 256), bf16), ((96, 1024), f32), ((8, 64, 1024), bf16)],
        who, part_no, tail_ctx, swap(tail_ctx[:, 128:, :128]), cond_act, ada, keep, swap(send),
    )
    tail, gm0 = lax.optimization_barrier((exchange(tail, "tp"), mixed0))
    (grad_act,) = run(k_cond_tp, [((8, 8, 1024), f32)], tail)
    grad_act = exchange(grad_act, "ctx")
    (ends,) = run(k_ends, [((LAT, 128, 1024), f32)], tail)

    (send,) = run(k_final_send, [((128, 768), bf16)], who, gm0, mixed)
    grad_up, grad_down, grad_qkv, grad_out = run(
        k_final,
        [((128, 512), f32), ((512, 128), f32), ((3, 128, 128), f32), ((128, 128), f32)],
        who, gm0, mixed, swap(send), ga0, swap(ga0),
    )
    classes = jnp.arange(label_table.shape[0], dtype=jnp.int32)[:, None]
    match = [classes == labels[l] for l in range(LAT)]
    slope = jax.nn.sigmoid(condition)
    slope = slope * (1.0 + condition * (1.0 - slope))
    grad_act, ends, grad_up, grad_down, grad_qkv, grad_out, match, slope = lax.optimization_barrier(
        (grad_act, ends, grad_up, grad_down, grad_qkv, grad_out, match, slope)
    )
    grad_act = grad_act.sum(axis=0)
    grad_cond = (grad_act + swap(grad_act))[:LAT] * slope
    grad_table = sum(jnp.where(match[l], grad_cond[l : l + 1], 0.0) for l in range(LAT))

    return (
        ends[None],
        grad_table,
        grad_ada.reshape(6, 16, width).transpose(2, 0, 1)[None],
        grad_qkv.transpose(1, 0, 2)[None],
        grad_out[None],
        grad_up[None],
        grad_down[None],
    )


def solution(mesh):
    return jax.shard_map(
        body,
        mesh=mesh,
        in_specs=(
            P(None, "ctx", None),
            P(None, "ctx", None),
            P(),
            P(),
            P(),
            P("pipe", None, None, ("ctx", "tp")),
            P("pipe", "ctx", None, "tp"),
            P("pipe", "tp", "ctx"),
            P("pipe", "ctx", "tp"),
            P("pipe", "tp", "ctx"),
        ),
        out_specs=(
            P("pipe", None, "ctx", None),
            P(),
            P("pipe", None, None, ("ctx", "tp")),
            P("pipe", "ctx", None, "tp"),
            P("pipe", "tp", "ctx"),
            P("pipe", "ctx", "tp"),
            P("pipe", "tp", "ctx"),
        ),
        check_vma=False,
    )
```

```python
import math

import jax
import jax.numpy as jnp
from jax import lax
from jax.experimental import pallas as pl
from jax.experimental.pallas import tpu as pltpu
from jax.sharding import PartitionSpec as P


LAT = 3
HEAD = 64
EPS = 1e-06
GELU_C = math.sqrt(2.0 / math.pi)
GELU_A = 0.044715
STORE_ROWS = 34048

f32 = jnp.float32
bf16 = jnp.bfloat16


def sds(shape, dtype):
    return jax.ShapeDtypeStruct(shape, dtype)


def up16(n):
    return -(-n // 16) * 16


class Slot:
    def __init__(self, row, shape, dtype):
        self.row, self.shape, self.dtype = row, shape, dtype
        self.rows = up16(shape[0]) * (2 if dtype == f32 else 1)

    def of(self, ref):
        return ref.at[pl.ds(self.row, self.rows), pl.ds(0, self.shape[1])]


class Store:
    def __init__(self):
        self.array, self.next = None, 0

    def slot(self, shape, dtype):
        s = Slot(self.next, shape, dtype)
        self.next += s.rows
        assert self.next <= STORE_ROWS
        return s


class Save:
    def __init__(self, array, slot):
        self.array, self.slot = array, slot


class Near:
    def __init__(self, array):
        self.array = array


class Half:
    def __init__(self, core, own, other, block, rows, at, width, slot):
        self.core, self.own, self.other = core, own, other
        self.block, self.rows, self.at, self.width, self.slot = block, rows, at, width, slot


class Held:
    def __init__(self, ref, wait, shape, dtype):
        self.ref, self.wait, self.shape, self.dtype = ref, wait, shape, dtype

    def ready(self):
        if self.wait is not None:
            self.wait()
            self.wait = None

    def __getitem__(self, at):
        self.ready()
        if self.dtype != f32 or self.ref.dtype == f32:
            return self.ref[at]
        n = self.shape[0]
        low = up16(n)
        return self.ref[:n].astype(f32) + self.ref[low : low + n].astype(f32)


class Kept:
    def __init__(self, ref, copy, shape, dtype):
        self.ref, self.copy, self.shape, self.dtype, self.gone = ref, copy, shape, dtype, False

    def send(self):
        if not self.gone:
            self.copy.start()
            self.gone = True

    def __setitem__(self, at, v):
        if self.dtype == f32:
            n = self.shape[0]
            low = up16(n)
            high = v.astype(bf16)
            self.ref[:n] = high
            self.ref[low : low + n] = (v - high.astype(f32)).astype(bf16)
            self.send()
        else:
            self.ref[at] = v
            if at is Ellipsis:
                self.send()


def ready(*refs):
    for r in refs:
        if isinstance(r, Held):
            r.ready()


def call(store, kernel, outs, *args, alone=False):
    vmem = pl.BlockSpec(memory_space=pltpu.VMEM)
    smem = pl.BlockSpec(memory_space=pltpu.SMEM)
    far = pl.BlockSpec(memory_space=pltpu.HBM)
    uses = any(isinstance(a, (Slot, Save, Half)) for a in args) or any(
        isinstance(o, Slot) for o in outs
    )
    flat, in_specs, plan, scratch = [], [], [], []

    def hold(shape, dtype):
        scratch.append(pltpu.VMEM(shape, dtype))
        return len(scratch) - 1

    for a in args:
        if isinstance(a, Slot):
            plan.append(("slot", a, hold((a.rows, a.shape[1]), bf16)))
        elif isinstance(a, Near):
            plan.append(("near", len(flat), hold(a.array.shape, a.array.dtype)))
            flat.append(a.array)
            in_specs.append(far)
        elif isinstance(a, Half):
            plan.append(("half", len(flat), hold(a.slot.shape, bf16), a))
            flat += [a.own, a.other]
            in_specs += [far, far]
        else:
            v = a.array if isinstance(a, Save) else a
            plan.append(("here", len(flat), a))
            flat.append(v)
            in_specs.append(smem if v.dtype == jnp.int32 else vmem)
    out_shape, out_specs, out_plan = [], [], []
    for o in outs:
        if isinstance(o, Slot):
            out_plan.append((o, hold((o.rows, o.shape[1]), bf16)))
        elif alone:
            out_plan.append((len(out_shape), hold(*o)))
            out_shape.append(sds(*o))
            out_specs.append(far)
        else:
            out_plan.append((None, len(out_shape)))
            out_shape.append(sds(*o))
            out_specs.append(vmem)
    n_args, n_out, n_hold = len(flat), len(out_shape), len(scratch)
    n_saves = sum(isinstance(a, (Save, Half)) for a in args)
    alias = {}
    if uses:
        if store.array is not None:
            flat.append(store.array)
            in_specs.append(far)
            alias = {len(flat) - 1: n_out}
        out_shape.append(sds((STORE_ROWS, 1024), bf16))
        out_specs.append(far)
    n_in = len(flat)
    n_sems = n_hold + n_saves

    def wrapped(*refs):
        ins, results = refs[:n_in], refs[n_in : n_in + len(out_shape)]
        holds = refs[n_in + len(out_shape) :]
        sems = holds[n_hold] if n_sems else None
        big = results[n_out] if uses else None
        given, leaving, late = [], [], n_hold
        for item in plan:
            if item[0] == "here":
                given.append(ins[item[1]])
                if isinstance(item[2], Save):
                    copy = pltpu.make_async_copy(ins[item[1]], item[2].slot.of(big), sems.at[late])
                    copy.start()
                    leaving.append(copy)
                    late += 1
                continue
            to, sem = holds[item[2]], sems.at[item[2]]
            if item[0] == "half":
                h = item[3]
                mine = lax.axis_index("pipe") == h.core
                for k in range(2):

                    @pl.when(mine if k == 0 else jnp.logical_not(mine))
                    def _(src=ins[item[1] + k]):
                        for c in range(h.slot.shape[0] // h.rows):
                            pltpu.make_async_copy(
                                src.at[pl.ds(c * h.block, h.rows), pl.ds(h.at, h.width)],
                                to.at[pl.ds(c * h.rows, h.rows)],
                                sem,
                            ).start()

                whole = pltpu.make_async_copy(to, to, sem)
                out = pltpu.make_async_copy(to, h.slot.of(big), sems.at[late])
                late += 1
                leaving.append(out)

                def arrive(whole=whole, out=out):
                    whole.wait()
                    out.start()

                given.append(Held(to, arrive, h.slot.shape, bf16))
                continue
            if item[0] == "slot":
                copy = pltpu.make_async_copy(item[1].of(big), to, sem)
                shape, dtype = item[1].shape, item[1].dtype
            else:
                copy = pltpu.make_async_copy(ins[item[1]], to, sem)
                shape, dtype = to.shape, to.dtype
            copy.start()
            given.append(Held(to, copy.wait, shape, dtype))
        for slot, at in out_plan:
            if slot is None:
                given.append(results[at])
            else:
                if isinstance(slot, Slot):
                    copy = pltpu.make_async_copy(holds[at], slot.of(big), sems.at[at])
                    kept = Kept(holds[at], copy, slot.shape, slot.dtype)
                else:
                    copy = pltpu.make_async_copy(holds[at], results[slot], sems.at[at])
                    kept = Kept(holds[at], copy, None, None)
                leaving.append(copy)
                given.append(kept)
        kernel(*given)
        ready(*given)
        for g in given:
            if isinstance(g, Kept):
                g.send()
        for copy in leaving:
            copy.wait()

    got = pl.pallas_call(
        wrapped,
        out_shape=tuple(out_shape),
        in_specs=in_specs,
        out_specs=tuple(out_specs),
        scratch_shapes=scratch + ([pltpu.SemaphoreType.DMA((n_sems,))] if n_sems else []),
        input_output_aliases=alias,
        compiler_params=pltpu.CompilerParams(vmem_limit_bytes=(60 if alone else 24) * 1024 * 1024),
    )(*flat)
    if uses:
        store.array = got[n_out]
    return got[:n_out]


def mm(a, b):
    return lax.dot_general(a, b, (((1,), (0,)), ((), ())), preferred_element_type=f32)


def mm_nt(a, b):
    return lax.dot_general(a, b, (((1,), (1,)), ((), ())), preferred_element_type=f32)


def mm_tn(a, b):
    return lax.dot_general(a, b, (((0,), (0,)), ((), ())), preferred_element_type=f32)


def part(mod, k):
    return jnp.concatenate(
        [jnp.broadcast_to(mod[3 * k + l : 3 * k + l + 1, :], (8, mod.shape[1])) for l in range(LAT)],
        axis=0,
    )


def centred(x):
    c = x - jnp.mean(x, axis=-1, keepdims=True)
    r = lax.rsqrt(jnp.mean(c * c, axis=-1, keepdims=True) + EPS)
    return c * r, r


def norm_back(x, dy, scale):
    xh, r = centred(x)
    g = dy * (1.0 + scale)
    dx = r * (
        g - jnp.mean(g, axis=-1, keepdims=True) - xh * jnp.mean(g * xh, axis=-1, keepdims=True)
    )
    return dx, dy, dy * xh


def row_sums(*vs):
    return jnp.concatenate(
        [jnp.sum(v[8 * l : 8 * l + 8], axis=0, keepdims=True) for v in vs for l in range(LAT)], axis=0
    )


def summed(ref, *at):
    total = ref[(0, *at)].astype(f32)
    for j in range(1, 8):
        total = total + ref[(j, *at)].astype(f32)
    return total


def to_all(ref, v):
    for j in range(8):
        ref[j] = v


def by_latent(v):
    v = v.reshape(8, LAT, 8, v.shape[-1])
    return [v[:, l].reshape(64, v.shape[-1]) for l in range(LAT)]


def rows_of(v):
    return v.reshape(-1, v.shape[-1])


def by_part(vs):
    w = vs[0].shape[-1]
    return jnp.stack([v.reshape(8, 8, w) for v in vs], axis=1).reshape(192, w)


def gelu_parts(x):
    t = jnp.tanh(GELU_C * (x + GELU_A * (x * x * x)))
    return t


def k_halves(p_ref, wq_ref, wo_ref, up_ref, down_ref, keep_ref, send_ref):
    ready(wq_ref, wo_ref, up_ref, down_ref)

    a = jnp.concatenate([wq_ref[0], wq_ref[1], up_ref[...]], axis=1).astype(f32)
    wo, down = wo_ref[...].astype(f32).T, down_ref[...].astype(f32).T
    b = jnp.concatenate([wq_ref[2].astype(f32), wo, down], axis=1)
    first = p_ref[0] == 0
    send_ref[...] = jnp.where(first, b, a).astype(bf16)
    keep_ref[...] = jnp.where(first, a, b).astype(bf16)


def k_pack(
    p_ref, t_ref, lab_ref, table_ref, sinus_ref, ada_ref, keep_ref, got_ref,
    o_ref, w0_ref, w1_ref, cond_ref, act_ref,
):
    first = p_ref[0] == 0
    keep, got = keep_ref[...].astype(f32), got_ref[...].astype(f32)
    w0 = jnp.where(first, keep, got).astype(bf16)
    w0_ref[...] = w0[:, 256:]
    w1_ref[...] = jnp.where(first, got, keep).astype(bf16)
    row = lax.broadcasted_iota(jnp.int32, (8, table_ref.shape[0]), 0)
    col = lax.broadcasted_iota(jnp.int32, (8, table_ref.shape[0]), 1)
    label = jnp.where(row == 0, lab_ref[0], jnp.where(row == 1, lab_ref[1], lab_ref[2]))
    cond = mm(jnp.where(col == label, 1.0, 0.0).astype(bf16), table_ref[...])[:LAT] + sinus_ref[...]
    cond_ref[...] = cond
    act = (cond / (1.0 + jnp.exp(-cond))).astype(bf16)
    act_ref[...] = act
    row = lax.broadcasted_iota(jnp.int32, (96, 768), 0)
    lane = lax.broadcasted_iota(jnp.int32, (96, 768), 1)
    to = 128 * (row // 16) + row % 16 + 16 * t_ref[0]
    place = jnp.where(lane == to, 1.0, 0.0).astype(bf16)
    mod = mm(mm_nt(act, ada_ref[...]).astype(bf16), place)
    mod = jnp.concatenate([mod[:, 128 * k : 128 * k + 128] for k in range(6)], axis=0)
    mod = jnp.concatenate([mod, jnp.zeros((14, 128), f32)], axis=0)
    mod = jnp.concatenate([mod, jnp.zeros((32, 128), f32)], axis=1).astype(bf16)
    for j in range(8):
        o_ref[j, :128] = w0[:, :256]
        o_ref[j, 128:] = mod


def k_spread(r_ref, o_ref):
    for c in range(8):
        v = r_ref[c, 128:, :128][:24]
        for j in range(8):
            o_ref[j, c] = v


def k_mods(r_ref, o_ref):
    for c in range(8):
        o_ref[:, 128 * c : 128 * c + 128] = summed(r_ref, c).astype(bf16)


def k_two_layers(p_ref, own_ref, other_ref, a_ref, b_ref):
    own, other, first = own_ref[...].astype(f32), other_ref[...].astype(f32), p_ref[0] == 0
    a_ref[...] = jnp.where(first, own, other).astype(bf16)
    b_ref[...] = jnp.where(first, other, own).astype(bf16)


def put_qkv(y, q_ref, kv_ref):
    y = jnp.concatenate(by_latent(y), axis=0).astype(bf16)
    q_ref[...] = y[:, :128]
    to_all(kv_ref, y[:, 128:])


def triple(n, wa_ref, wb_ref):
    a = mm(n, rows_of(wa_ref[...]))
    return jnp.concatenate([a, mm(n, rows_of(wb_ref[...])[:, :128])], axis=1)


def k_rows(p_ref, t_ref, x_ref, c_ref, x_all_ref, x_own_ref, c_all_ref, c_own_ref):
    start = pl.multiple_of(64 * p_ref[0], 64)
    few = pl.multiple_of(64 * p_ref[0] + 8 * t_ref[0], 8)
    ready(x_ref, c_ref)
    for ref, all_ref, own_ref in ((x_ref.ref, x_all_ref, x_own_ref), (c_ref.ref, c_all_ref, c_own_ref)):
        blocks = [ref[l, pl.ds(start, 64), :] for l in range(LAT)]
        all_ref[...] = jnp.concatenate(
            [b[8 * j : 8 * j + 8] for j in range(8) for b in blocks], axis=0
        )
        own_ref[...] = jnp.concatenate([ref[l, pl.ds(few, 8), :] for l in range(LAT)], axis=0)


def k_first(x_ref, mod_ref, wa_ref, wb_ref, n_ref, q_ref, kv_ref):
    mod = mod_ref[...].astype(f32)
    shift, scale = part(mod, 0), 1.0 + part(mod, 1)
    x = x_ref[...]
    rows = [centred(x[24 * j : 24 * j + 24])[0] * scale + shift for j in range(8)]
    n = jnp.concatenate(rows, axis=0).astype(bf16)
    n_ref[...] = n
    put_qkv(triple(n, wa_ref, wb_ref), q_ref, kv_ref)


def k_qkv(n_ref, wa_ref, wb_ref, q_ref, kv_ref):
    put_qkv(triple(n_ref[...], wa_ref, wb_ref), q_ref, kv_ref)


def head_rows(v):
    lane = lax.broadcasted_iota(jnp.int32, v.shape, 1)
    zero = jnp.zeros_like(v)
    return jnp.concatenate(
        [jnp.where(lane < HEAD, v, zero), jnp.where(lane < HEAD, zero, v)], axis=0
    )


def head_lanes(v):
    lane = lax.broadcasted_iota(jnp.int32, (64, 128), 1)
    return jnp.where(lane < HEAD, v[:64], v[64:])


def keys_values(a_ref, b_ref, l):
    at = [64 * (LAT * c + l) for c in range(8)]
    kv = jnp.concatenate([r[i : i + 64] for r in (a_ref, b_ref) for i in at], axis=0)
    return kv[:, :128], kv[:, 128:]


def soft(qs, k):
    s = mm_nt(k, qs) * 0.125
    e = jnp.exp(s - jnp.max(s, axis=0, keepdims=True))
    return e * (1.0 / jnp.sum(e, axis=0, keepdims=True))


def k_attn(q_ref, a_ref, b_ref, w_ref, att_ref, o_ref):
    outs = []
    for l in range(LAT):
        k, v = keys_values(a_ref, b_ref, l)
        probs = soft(head_rows(q_ref[64 * l : 64 * l + 64].astype(f32)).astype(bf16), k)
        outs.append(head_lanes(mm_tn(probs.astype(bf16), v)))
    att = by_part(outs).astype(bf16)
    att_ref[...] = att
    o_ref[...] = mm_nt(att, rows_of(w_ref[...])[:, 128:]).astype(bf16)


def k_attn_back(q_ref, a_ref, b_ref, w_ref, db_ref, dq_ref, da_ref, dp_ref):
    datt = by_latent(mm(db_ref[...], rows_of(w_ref[...])[:, 128:]))
    for l in range(LAT):
        k, v = keys_values(a_ref, b_ref, l)
        qs = head_rows(q_ref[64 * l : 64 * l + 64].astype(f32)).astype(bf16)
        do = head_rows(datt[l]).astype(bf16)
        probs = soft(qs, k)
        dprobs = mm_nt(v, do)
        dv = mm(probs.astype(bf16), do)
        ds = probs * (dprobs - jnp.sum(probs * dprobs, axis=0, keepdims=True))
        ds = ds.astype(bf16)
        dk = mm(ds, qs) * 0.125
        dq_ref[64 * l : 64 * l + 64] = (head_lanes(mm_tn(ds, k)) * 0.125).astype(bf16)
        dkv = jnp.concatenate([dk, dv], axis=1).astype(bf16)
        for c in range(8):
            at = 64 * (LAT * c + l)
            da_ref[at : at + 64] = dkv[64 * c : 64 * c + 64]
            dp_ref[at : at + 64] = dkv[512 + 64 * c : 512 + 64 * c + 64]


def k_pair_sum(a_ref, b_ref, o_ref):
    o_ref[...] = (a_ref[...].astype(f32) + b_ref[...].astype(f32)).astype(bf16)


def k_qkv_back(dq_ref, r_ref, wa_ref, wb_ref, dt_ref, o_ref):
    dt = jnp.concatenate([dq_ref[...].astype(f32), summed(r_ref)], axis=1)
    dt = by_part([dt[64 * l : 64 * l + 64] for l in range(LAT)]).astype(bf16)
    dt_ref[...] = dt
    back = mm_nt(dt[:, :256], rows_of(wa_ref[...])) + mm_nt(dt[:, 256:], rows_of(wb_ref[...])[:, :128])
    o_ref[...] = back.astype(bf16)


def k_mid(r_ref, x_ref, mod_ref, br_ref, mid_ref, o_ref):
    mod = mod_ref[...].astype(f32)
    branch = summed(r_ref)
    mid = x_ref[...] + part(mod, 2) * branch
    br_ref[...] = branch
    mid_ref[...] = mid
    xh, _ = centred(mid)
    to_all(o_ref, (xh * (1.0 + part(mod, 4)) + part(mod, 3)).astype(bf16))


def k_mlp(n_ref, up_ref, down_ref, hid_ref, o_ref):
    pre = mm(n_ref[...], rows_of(up_ref[...]))
    hid = (0.5 * pre * (1.0 + gelu_parts(pre))).astype(bf16)
    hid_ref[...] = hid
    o_ref[...] = mm_nt(hid, rows_of(down_ref[...])).astype(bf16)


def gelu_slope(pre, t):
    inner = GELU_C * (1.0 + 3.0 * GELU_A * pre * pre)
    return 0.5 * (1.0 + t) + 0.5 * pre * (1.0 - t * t) * inner


def k_mlp_both(n_ref, up_ref, down_ref, dm_ref, hid_ref, dpre_ref, o_ref):
    pre = mm(n_ref[...], rows_of(up_ref[...]))
    t = gelu_parts(pre)
    hid = (0.5 * pre * (1.0 + t)).astype(bf16)
    hid_ref[...] = hid
    out = mm_nt(hid, rows_of(down_ref[...])).astype(bf16)
    dhid = mm(dm_ref[...], rows_of(down_ref[...]))
    dpre = (dhid * gelu_slope(pre, t)).astype(bf16)
    dpre_ref[...] = dpre
    back = mm_nt(dpre, rows_of(up_ref[...])).astype(bf16)
    for j in range(8):
        o_ref[j, 0] = out[24 * j : 24 * j + 24]
        o_ref[j, 1] = back[24 * j : 24 * j + 24]


def k_mlp_back(n_ref, up_ref, down_ref, dm_ref, dpre_ref, o_ref):
    pre = mm(n_ref[...], rows_of(up_ref[...]))
    dhid = mm(dm_ref[...], rows_of(down_ref[...]))
    dpre = (dhid * gelu_slope(pre, gelu_parts(pre))).astype(bf16)
    dpre_ref[...] = dpre
    o_ref[...] = mm_nt(dpre, rows_of(up_ref[...])).astype(bf16)


def k_gate_rows(c_ref, mod_ref, o_ref):
    gate = part(mod_ref[...].astype(f32), 5)
    c = c_ref[...]
    rows = [gate * c[24 * j : 24 * j + 24] for j in range(8)]
    o_ref[...] = jnp.concatenate(rows, axis=0).astype(bf16)


def k_next(r_ref, mid_ref, mod_ref, mod_next_ref, mlp_ref, x_ref, o_ref):
    mod, mod_next = mod_ref[...].astype(f32), mod_next_ref[...].astype(f32)
    mlp = summed(r_ref)
    mlp_ref[...] = mlp
    x = mid_ref[...] + part(mod, 5) * mlp
    x_ref[...] = x
    xh, _ = centred(x)
    to_all(o_ref, (xh * (1.0 + part(mod_next, 1)) + part(mod_next, 0)).astype(bf16))


def back_two(mod, mid, branch, dy, dn, mlp, dmid_ref, dmod_ref, o_ref):
    dx, ds, dc = norm_back(mid, dn, part(mod, 4))
    dmid = dy + dx
    dmid_ref[...] = dmid
    to_all(o_ref, (part(mod, 2) * dmid).astype(bf16))
    dmod_ref[...] = row_sums(dmid * branch, ds, dc, dy * mlp)


def k_last(r_ref, mid_ref, br_ref, dy_ref, mod_ref, res_ref, dmid_ref, dmod_ref, o_ref):
    mod = mod_ref[...].astype(f32)
    mlp, dn = summed(r_ref, 0), summed(r_ref, 1)
    mid = mid_ref[...]
    res_ref[...] = mid + part(mod, 5) * mlp
    back_two(mod, mid, br_ref[...], dy_ref[...], dn, mlp, dmid_ref, dmod_ref, o_ref)


def k_back_two(r_ref, mid_ref, br_ref, dy_ref, mlp_ref, mod_ref, dmid_ref, dmod_ref, o_ref):
    mod = mod_ref[...].astype(f32)
    back_two(
        mod, mid_ref[...], br_ref[...], dy_ref[...], summed(r_ref), mlp_ref[...],
        dmid_ref, dmod_ref, o_ref,
    )


def k_back_one(r_ref, x_ref, dmid_ref, mod_ref, mod_before_ref, dx_ref, dmod_ref, o_ref):
    dx, ds, dc = norm_back(x_ref[...], summed(r_ref), part(mod_ref[...].astype(f32), 1))
    dx = dmid_ref[...] + dx
    dx_ref[...] = dx
    dmod_ref[...] = row_sums(ds, dc)
    to_all(o_ref, (part(mod_before_ref[...].astype(f32), 5) * dx).astype(bf16))


def k_early(p_ref, d0_ref, d1a_ref, d1b_ref, keep_ref, send_ref):
    first = p_ref[0] == 0
    none = jnp.zeros((6, keep_ref.shape[1]), f32)
    d0 = jnp.concatenate([none, d0_ref[...]], axis=0)
    d1 = jnp.concatenate([d1b_ref[...], d1a_ref[...]], axis=0)
    keep_ref[...] = jnp.where(first, d0, d1)
    send_ref[...] = jnp.where(first, d1, d0)


def k_qkv_back_first(dq_ref, r_ref, wa_ref, wb_ref, x_ref, keep_ref, got_ref, dt_ref, o_ref):
    dt = jnp.concatenate([dq_ref[...].astype(f32), summed(r_ref)], axis=1)
    dt = by_part([dt[64 * l : 64 * l + 64] for l in range(LAT)]).astype(bf16)
    dt_ref[...] = dt
    back = mm_nt(dt[:, :256], rows_of(wa_ref[...])) + mm_nt(dt[:, 256:], rows_of(wb_ref[...])[:, :128])
    x = x_ref[...]
    ds = jnp.zeros((24, x.shape[1]), f32)
    dc = jnp.zeros((24, x.shape[1]), f32)
    for j in range(8):
        dn = back[24 * j : 24 * j + 24]
        ds = ds + dn
        dc = dc + dn * centred(x[24 * j : 24 * j + 24])[0]
    sums = jnp.concatenate([row_sums(ds, dc), keep_ref[...] + got_ref[...]], axis=0)
    for j in range(8):
        o_ref[j] = jnp.concatenate([back[24 * j : 24 * j + 24], sums], axis=0).astype(bf16)


def rows_sum(r_ref, at, n):
    total = r_ref[0].astype(f32)[at : at + n]
    for j in range(1, 8):
        total = total + r_ref[j].astype(f32)[at : at + n]
    return total


def k_back_first(p_ref, r_ref, x_ref, dmid_ref, mod_ref, res_ref, keep_ref, send_ref):
    first = p_ref[0] == 0
    dn = rows_sum(r_ref, 0, 24)
    dx, _, _ = norm_back(x_ref[...], dn, part(mod_ref[...].astype(f32), 1))
    dx = dmid_ref[...] + dx
    res = res_ref[...]
    keep_ref[...] = jnp.where(first, dx, res)
    send_ref[...] = jnp.where(first, res, dx)


def k_tail_ctx(r_ref, a_ref, b_ref, o_ref):
    total = rows_sum(r_ref, 24, 24)
    total = jnp.concatenate([total, jnp.zeros((8, total.shape[1]), f32)], axis=0).astype(bf16)
    none = jnp.zeros((32, 128), bf16)
    for c in range(8):
        at = slice(128 * c, 128 * c + 128)
        o_ref[c, :128, :] = (a_ref[at].astype(f32) + b_ref[at].astype(f32)).astype(bf16)
        o_ref[c, 128:, :128] = total[:, at]
        o_ref[c, 128:, 128:] = none


def k_ends(r_ref, o_ref):
    for j in range(8):
        v = r_ref[j].astype(f32)
        for half in range(2):
            for l in range(LAT):
                at = 64 * half + 8 * j
                o_ref[l, at : at + 8, :] = v[24 * half + 8 * l : 24 * half + 8 * l + 8]


def k_cond(
    p_ref, t_ref, r_ref, other_ref, act_ref, ada_ref, keep_ref, got_ref, g_ref, ada_grad_ref, o_ref
):
    first = p_ref[0] == 0
    total = summed(r_ref)
    d = total[128:, :128]
    late = jnp.where(first, d[:6] + summed(other_ref)[:6], 0.0)
    d = jnp.concatenate([d[6:12] + late, d[12:24], jnp.zeros((14, 128), f32)], axis=0)
    lane = lax.broadcasted_iota(jnp.int32, (128, 16), 0)
    col = lax.broadcasted_iota(jnp.int32, (128, 16), 1)
    pick = jnp.where(lane == col + 16 * t_ref[0], 1.0, 0.0).astype(bf16)
    d = mm(d.astype(bf16), pick)
    act = act_ref[...]
    c = jnp.zeros(act.shape, f32)
    for k in range(6):
        dk = d[3 * k : 3 * k + 3].astype(bf16)
        ada_grad_ref[16 * k : 16 * k + 16, :] = mm_tn(dk, act)
        c = c + mm(dk, ada_ref[16 * k : 16 * k + 16, :])
    keep, got = keep_ref[...], got_ref[...]
    v = [jnp.where(first, keep, got), jnp.where(first, got, keep), c, jnp.zeros((5, c.shape[1]), f32)]
    to_all(o_ref, jnp.concatenate(v, axis=0).astype(bf16))
    g_ref[...] = total[:128].astype(bf16)


def k_cond_tp(r_ref, o_ref):
    to_all(o_ref, rows_sum(r_ref, 48, 8))


def k_final_send(p_ref, m0_ref, m1_ref, o_ref):
    m0, m1 = m0_ref[...].astype(f32), m1_ref[...].astype(f32)
    o_ref[:, :512] = jnp.where(p_ref[0] == 0, m1[:, :512], m0).astype(bf16)
    o_ref[:, 512:] = m1[:, 512:].astype(bf16)


def k_final(p_ref, m0_ref, m1_ref, a_ref, g_ref, b_ref, up_ref, down_ref, qkv_ref, out_ref):
    first = p_ref[0] == 0
    m0, m1, a = (r[...].astype(f32) for r in (m0_ref, m1_ref, a_ref))
    g, b = g_ref[...].astype(f32), b_ref[...].astype(f32)
    up_ref[...] = jnp.where(first, m0, a[:, :512])
    down_ref[...] = jnp.where(first, a[:, :512], m1[:, :512]).T
    qk = jnp.where(first, g, a[:, 512:])
    vo = jnp.where(first, b, m1[:, 512:])
    qkv_ref[0], qkv_ref[1], qkv_ref[2] = qk[:, :128], qk[:, 128:], vo[:, :128]
    out_ref[...] = vo[:, 128:].T


def k_grad_mlp(p_ref, n_ref, dpre_ref, dm_ref, hid_ref, keep_ref, send_ref):
    first = p_ref[0] == 0
    n, dm = n_ref[...], dm_ref[...]
    dpre, hid = dpre_ref[...], hid_ref[...]

    def pick(a, b):
        return jnp.where(first, a.astype(f32), b.astype(f32)).astype(bf16)

    send_ref[...] = mm_tn(pick(dm, n), pick(hid, dpre)).astype(bf16)
    keep_ref[...] = mm_tn(pick(n, dm), pick(dpre, hid)).astype(bf16)


def k_grad_attn(p_ref, n_ref, dt_ref, db_ref, att_ref, keep_ref, send_ref):
    first = p_ref[0] == 0
    n, dt = n_ref[...], dt_ref[...]
    qk = mm_tn(n, dt[:, :256])
    vo = jnp.concatenate([mm_tn(n, dt[:, 256:]), mm_tn(db_ref[...], att_ref[...])], axis=1)
    send_ref[...] = jnp.where(first, vo, qk).astype(bf16)
    keep_ref[...] = jnp.where(first, qk, vo).astype(bf16)


def k_grad_sum(*refs):
    o_ref, at = refs[-1], 0
    for keep, got in zip(refs[0:-1:2], refs[1:-1:2]):
        v = (keep[...].astype(f32) + got[...].astype(f32)).astype(bf16)
        o_ref[:, at : at + v.shape[1]] = v
        at += v.shape[1]


def exchange(x, axis):
    return lax.all_to_all(x, axis, 0, 0, tiled=True)


def swap(x):
    return lax.ppermute(x, "pipe", [(0, 1), (1, 0)])


def body(latents, cotangent, labels, steps, label_table, w_ada, w_qkv, w_out, w_up, w_down):
    p, t = lax.axis_index("pipe"), lax.axis_index("tp")
    who, part_no = p.astype(jnp.int32).reshape(1), t.astype(jnp.int32).reshape(1)
    width = latents.shape[2]

    store = Store()
    slot = store.slot

    def run(kernel, outs, *args, alone=False):
        return call(store, kernel, outs, *args, alone=alone)

    keep, send = run(
        k_halves, [((128, 768), bf16)] * 2,
        who, Near(w_qkv[0].transpose(1, 0, 2)), Near(w_out[0]), Near(w_up[0]), Near(w_down[0]),
        alone=True,
    )
    half = width // 2
    freq = jnp.exp(-math.log(10000.0) * jnp.arange(half, dtype=f32) / half)
    angles = steps.astype(f32)[:, None] * freq[None, :]
    sinus = jnp.concatenate([jnp.cos(angles), jnp.sin(angles)], axis=1)
    ada = w_ada[0].transpose(1, 2, 0).reshape(96, width)
    packed, w0, w1, condition, cond_act = run(
        k_pack,
        [
            ((8, 160, 256), bf16), ((128, 512), bf16), ((128, 768), bf16),
            ((LAT, width), f32), ((LAT, width), bf16),
        ],
        who, part_no, labels, Near(label_table), Near(sinus), Near(ada), Near(keep), Near(swap(send)),
        alone=True,
    )
    w0 = lax.all_gather(w0, "ctx", axis=0, tiled=True)
    packed = exchange(packed, "ctx")
    packed, latents, cotangent = lax.optimization_barrier((packed, latents, cotangent))
    (spread,) = run(k_spread, [((8, 8, 24, 128), bf16)], packed)
    packed = packed.reshape(1280, 256)
    packed_other = swap(packed)
    sa = [[slot((1024, 256), bf16) for _ in range(2)] for _ in range(2)]
    sm = [[slot((1024, 512), bf16) for _ in range(2)] for _ in range(2)]
    wa0 = [Half(c, packed, packed_other, 160, 128, 0, 256, sa[0][c]) for c in range(2)]
    x_all, x0 = slot((192, 1024), f32), slot((24, 1024), f32)
    cot_all, cot = slot((192, 1024), f32), slot((24, 1024), f32)
    run(k_rows, [x_all, x0, cot_all, cot], who, part_no, Near(latents), Near(cotangent), alone=True)
    spread, store.array = lax.optimization_barrier((exchange(spread, "tp"), store.array))
    (mod_own,) = run(k_mods, [((24, 1024), bf16)], spread)
    mods = run(k_two_layers, [((24, 1024), bf16)] * 2, who, mod_own, swap(mod_own))

    bc = ((8, 24, 1024), bf16)
    wide = ((192, 1024), bf16)
    kv_all = ((1536, 256), bf16)

    def rows24(n=24):
        return slot((n, 1024), f32)

    def rows192(n):
        return slot((192, n), bf16)

    def attn_forward(q, kv, w):
        kv_a = exchange(kv, "ctx").reshape(1536, 256)
        kv_b = swap(kv_a)
        att, sa, sb = rows192(128), slot((1536, 256), bf16), slot((1536, 256), bf16)
        (branch,) = run(k_attn, [att, wide], q, Save(kv_a, sa), Save(kv_b, sb), w[1])
        return (q, sa, sb, att), exchange(branch.reshape(8, 24, 1024), "tp")

    def attn_back(kept, normed, dbranch, w, last=None):
        q, kv_a, kv_b, att = kept
        db, dq, dt = rows192(1024), rows192(128), rows192(384)
        da, dp = run(k_attn_back, [dq, kv_all, kv_all], q, kv_a, kv_b, w[1], Save(dbranch, db))
        (both,) = run(k_pair_sum, [kv_all], da, swap(dp))
        arrived = exchange(both.reshape(8, 192, 256), "ctx")
        if last is None:
            (dn,) = run(k_qkv_back, [dt, wide], dq, arrived, *w)
            dn = dn.reshape(8, 24, 1024)
        else:
            (dn,) = run(k_qkv_back_first, [dt, ((8, 48, 1024), bf16)], dq, arrived, *w, *last)
        arrived = exchange(dn, "tp")
        keep = slot((1024, 256), bf16)
        (send,) = run(k_grad_attn, [keep, ((1024, 256), bf16)], who, normed, dt, db, att)
        return arrived, (keep, swap(send))

    def grads_mlp(n, dpre, dm, hid):
        keep = slot((1024, 512), bf16)
        (send,) = run(k_grad_mlp, [keep, ((1024, 512), bf16)], who, n, dpre, dm, hid)
        return keep, send

    def to_rows(x):
        return exchange(x, "tp").reshape(192, 1024)

    normed0, q0, dm1 = rows192(1024), rows192(128), rows192(1024)
    (kv,) = run(k_first, [normed0, q0, ((8, 192, 256), bf16)], x_all, mods[0], *wa0)
    wa0 = sa[0]
    run(k_gate_rows, [dm1], cot_all, mods[1])
    kept0, arrived = attn_forward(q0, kv, wa0)
    br0, mid0 = rows24(), rows24()
    (n2,) = run(k_mid, [br0, mid0, bc], arrived, x0, mods[0])
    n2 = to_rows(n2)
    w0_other = swap(w0)
    wm0 = [Half(c, w0, w0_other, 1024, 1024, 0, 512, sm[0][c]) for c in range(2)]
    n2_0, hid0 = rows192(1024), rows192(512)
    (out,) = run(k_mlp, [hid0, wide], Save(n2, n2_0), *wm0)
    wm0 = sm[0]
    arrived = exchange(out.reshape(8, 24, 1024), "tp")
    mlp0, x1 = rows24(), rows24()
    (n1,) = run(k_next, [mlp0, x1, bc], arrived, mid0, mods[0], mods[1])

    w1 = lax.all_gather(w1, "ctx", axis=0, tiled=True)
    n1, w1 = lax.optimization_barrier((n1, w1))
    n1 = to_rows(n1)
    w1_other = swap(w1)
    wa1 = [Half(c, w1, w1_other, 1024, 1024, 0, 256, sa[1][c]) for c in range(2)]
    wm1 = [Half(c, w1, w1_other, 1024, 1024, 256, 512, sm[1][c]) for c in range(2)]
    normed1, q1 = rows192(1024), rows192(128)
    (kv,) = run(k_qkv, [q1, ((8, 192, 256), bf16)], Save(n1, normed1), *wa1)
    wa1 = sa[1]
    kept1, arrived = attn_forward(q1, kv, wa1)
    br1, mid1 = rows24(), rows24()
    (n2,) = run(k_mid, [br1, mid1, bc], arrived, x1, mods[1])
    n2 = to_rows(n2)
    n2_1, hid1, dpre1 = rows192(1024), rows192(512), rows192(512)
    (both,) = run(
        k_mlp_both, [hid1, dpre1, ((8, 2, 24, 1024), bf16)], Save(n2, n2_1), *wm1, dm1
    )
    arrived = exchange(both, "tp")
    res1, dmid1, dmod1a = rows24(), rows24(), rows24(12)
    (db,) = run(k_last, [res1, dmid1, dmod1a, bc], arrived, mid1, br1, cot, mods[1])
    gm1, send = grads_mlp(n2_1, dpre1, dm1, hid1)
    gm1 = gm1, swap(send)

    arrived, ga1 = attn_back(kept1, normed1, to_rows(db), wa1)
    dx1, dmod1b = rows24(), rows24(6)
    (dm,) = run(k_back_one, [dx1, dmod1b, bc], arrived, x1, dmid1, mods[1], mods[0])
    (mixed,) = run(k_grad_sum, [((1024, 768), bf16)], *gm1, *ga1)
    mixed = lax.psum_scatter(mixed, "ctx", tiled=True)
    dm = to_rows(dm)

    dm0, dpre0 = rows192(1024), rows192(512)
    (dn,) = run(k_mlp_back, [dpre0, wide], n2_0, *wm0, Save(dm, dm0))
    arrived = exchange(dn.reshape(8, 24, 1024), "tp")
    gm0, send = grads_mlp(n2_0, dpre0, dm0, hid0)
    dmid0, dmod0a = rows24(), rows24(12)
    (db,) = run(k_back_two, [dmid0, dmod0a, bc], arrived, mid0, br0, dx1, mlp0, mods[0])
    db, send = lax.optimization_barrier((db, send))
    (mixed0,) = run(k_grad_sum, [((1024, 512), bf16)], gm0, swap(send))
    mixed0 = lax.psum_scatter(mixed0, "ctx", tiled=True)
    keep, send = run(k_early, [((18, 1024), f32)] * 2, who, dmod0a, dmod1a, dmod1b)
    arrived, ga0 = attn_back(kept0, normed0, to_rows(db), wa0, (x_all, keep, swap(send)))
    arrived, mixed = lax.optimization_barrier((arrived, mixed))

    (tail_ctx,) = run(k_tail_ctx, [((8, 160, 256), bf16)], arrived, *ga0)
    keep, send = run(
        k_back_first, [((24, 1024), f32)] * 2, who, arrived, x0, dmid0, mods[0], res1
    )
    tail_ctx = exchange(tail_ctx, "ctx")
    ga0, grad_ada, tail = run(
        k_cond, [((128, 256), bf16), ((96, 1024), f32), ((8, 56, 1024), bf16)],
        who, part_no, tail_ctx, swap(tail_ctx[:, 128:, :128]), cond_act, ada, keep, swap(send),
    )
    tail, gm0 = exchange(tail, "tp"), mixed0
    (grad_act,) = run(k_cond_tp, [((8, 8, 1024), f32)], tail)
    grad_act = exchange(grad_act, "ctx")
    (ends,) = run(k_ends, [((LAT, 128, 1024), f32)], tail)

    (send,) = run(k_final_send, [((128, 768), bf16)], who, gm0, mixed)
    grad_up, grad_down, grad_qkv, grad_out = run(
        k_final,
        [((128, 512), f32), ((512, 128), f32), ((3, 128, 128), f32), ((128, 128), f32)],
        who, gm0, mixed, swap(send), ga0, swap(ga0),
    )
    classes = jnp.arange(label_table.shape[0], dtype=jnp.int32)[:, None]
    match = [classes == labels[l] for l in range(LAT)]
    slope = jax.nn.sigmoid(condition)
    slope = slope * (1.0 + condition * (1.0 - slope))
    grad_act, ends, grad_up, grad_down, grad_qkv, grad_out, match, slope = lax.optimization_barrier(
        (grad_act, ends, grad_up, grad_down, grad_qkv, grad_out, match, slope)
    )
    grad_act = grad_act.sum(axis=0)
    grad_cond = (grad_act + swap(grad_act))[:LAT] * slope
    grad_table = sum(jnp.where(match[l], grad_cond[l : l + 1], 0.0) for l in range(LAT))

    return (
        ends[None],
        grad_table,
        grad_ada.reshape(6, 16, width).transpose(2, 0, 1)[None],
        grad_qkv.transpose(1, 0, 2)[None],
        grad_out[None],
        grad_up[None],
        grad_down[None],
    )


def solution(mesh):
    return jax.shard_map(
        body,
        mesh=mesh,
        in_specs=(
            P(None, "ctx", None),
            P(None, "ctx", None),
            P(),
            P(),
            P(),
            P("pipe", None, None, ("ctx", "tp")),
            P("pipe", "ctx", None, "tp"),
            P("pipe", "tp", "ctx"),
            P("pipe", "ctx", "tp"),
            P("pipe", "tp", "ctx"),
        ),
        out_specs=(
            P("pipe", None, "ctx", None),
            P(),
            P("pipe", None, None, ("ctx", "tp")),
            P("pipe", "ctx", None, "tp"),
            P("pipe", "tp", "ctx"),
            P("pipe", "ctx", "tp"),
            P("pipe", "tp", "ctx"),
        ),
        check_vma=False,
    )
```
